32 devices in a mesh: tile: 16 (over z, y, x), band: 2 (over core).
Axes of the slice: x: 2, y: 2, z: 4, core: 2. Of those that a mesh axis runs over, the one named last changes fastest.
Arguments:
- concentration: float32 [4, 24, 128, 512], P(None, 'band', 'tile'), may hold values from -6 to 6
- adjoint_later: float32 [4, 24, 128, 512], P(None, 'band', 'tile'), may hold values from -6 to 6
- courant_east: float32 [24, 128, 512], P('band', 'tile'), may hold values from -0.25 to 0.25
- courant_north: float32 [24, 128, 512], P('band', 'tile'), may hold values from -0.25 to 0.25
- diffusivity: float32 [24, 128, 512], P('band', 'tile'), may hold values from 1 to 100
- tracer_factor: float32 [4], replicated, may hold values from 0.5 to 2
- sounding_cell: int32 [4096], P('tile'), may hold values from -1 to 4095, as said below
- sounding_value: float32 [4096], P('tile'), may hold values from -6 to 6
- sounding_precision: float32 [4096], P('tile'), may hold values from 0.2 to 2
- sounding_weight: float32 [4096, 24], P('tile', 'band')
Outputs:
- adjoint_earlier: float32 [4, 24, 128, 512], P(None, 'band', 'tile')
The draws below stay inside these ranges and needn't reach their ends.
Inputs may be any that keep to these rules, and one draw needn't show every extreme that they name: `sounding_cell`: slots come in blocks of 16, one block for each pair of owner and tile (tile = block index modulo 16); in a block the live slots come first and the rest hold -1. Every owner fills at least one block completely, and one tile receives full blocks from every owner.
All inputs are finite; a program needn't handle non-finite values.
Results may differ from the reference program's by a relative error of at most 0.0003.
Values sent between devices are 32-bit elements; how exact they have to be, the bound alone decides.
No kernel may reach another device: no remote copies, remote signals or barrier semaphores. Data moves between devices by JAX's collectives and lax.ppermute only.
A program may use at most 64 MiB of HBM per device.

```python
import math
import jax
import jax.numpy as jnp
from jax import lax

TR = 4
CX = 8
CY = 512
CAP = 16
STEPS = 2
LEV = 24
NX = 128
NY = 512
SLOTS = 4096
N_TILE = 16


def draw_sounding_cell(key, part):
    keys = jax.random.split(jax.random.fold_in(key, 11), 4)
    counts = jax.random.randint(keys[0], (N_TILE, N_TILE), 0, CAP + 1)
    full_tile = jax.random.randint(keys[1], (), 0, N_TILE)
    owner_pick = jax.random.randint(keys[2], (N_TILE,), 0, N_TILE)
    destination = jnp.arange(N_TILE)[None, :]
    counts = jnp.where((destination == full_tile) | (destination == owner_pick[:, None]), CAP, counts)
    position = jnp.arange(CAP)[None, None, :]
    cells = jax.random.randint(keys[3], (N_TILE, N_TILE, CAP), 0, CX * CY)
    return jnp.where(position < counts[:, :, None], cells, -1).reshape(-1).astype(jnp.int32)


def draw_sounding_weight(key, part):
    levels = jnp.arange(LEV, dtype=jnp.float32) / (LEV - 1)
    base = jnp.clip(jax.random.normal(jax.random.fold_in(key, 23), (SLOTS, LEV)), -4.0, 4.0)
    rising = 0.5 + levels
    return (base * rising[None, :] / math.sqrt(LEV)).astype(jnp.float32)


def level_of(rng, dims, pieces, low, top_value):
    factor_of = 1.0
    for dim, blocks in pieces:
        steps = jax.random.uniform(jax.random.fold_in(jax.random.fold_in(rng, 6), dim), (blocks,), jnp.float32, low / len(pieces), top_value / len(pieces))
        factor_of = factor_of * jnp.repeat(jnp.exp(steps), dims[dim] // blocks).reshape((-1,) + (1,) * (len(dims) - 1 - dim))
    return factor_of


def noise(key, extent, width, limit, cuts=(), kind=jnp.bfloat16):
    gain = level_of(key, extent, cuts, -0.22, 0.18) if cuts else 1.0
    drawn = jax.random.normal(key, extent, jnp.float32) * width * gain
    return jnp.minimum(jnp.maximum(drawn, -limit), limit).astype(kind)


def setup_inputs(seed: int = 0) -> dict:
    key_of = jax.random.split(jax.random.key(seed), 11)
    concentration = noise(key_of[0], (TR, LEV, NX, NY), 1.0, 6.0, ((1, 2), (2, 16)), jnp.float32)
    adjoint_later = noise(key_of[1], (TR, LEV, NX, NY), 1.0, 6.0, ((1, 2), (2, 16)), jnp.float32)
    courant_east = jnp.clip(jax.random.uniform(key_of[2], (LEV, NX, NY), jnp.float32, -0.25, 0.25) * level_of(key_of[2], (LEV, NX, NY), ((0, 2), (1, 16)), -0.4, 0.0), -0.25, 0.25)
    courant_north = jnp.clip(jax.random.uniform(key_of[3], (LEV, NX, NY), jnp.float32, -0.25, 0.25) * level_of(key_of[3], (LEV, NX, NY), ((0, 2), (1, 16)), -0.4, 0.0), -0.25, 0.25)
    diffusivity = jnp.clip(jnp.exp(math.log(100.0) - 4.6051702 * jax.random.uniform(key_of[4], (LEV, NX, NY), jnp.float32) ** level_of(key_of[4], (LEV, NX, NY), ((0, 2), (1, 16)), -0.2, 0.2)), 1.0, 100.0)
    tracer_factor = jnp.clip(jnp.exp(jax.random.uniform(key_of[5], (TR,), jnp.float32, math.log(0.5), math.log(2.0))), 0.5, 2.0)
    sounding_cell = draw_sounding_cell(jax.random.fold_in(key_of[10], 71), 0)
    sounding_value = noise(key_of[7], (SLOTS,), 1.0, 6.0, ((0, 16),), jnp.float32)
    sounding_precision = jnp.clip(jnp.exp(math.log(2.0) - 2.3025851 * jax.random.uniform(key_of[8], (SLOTS,), jnp.float32) ** level_of(key_of[8], (SLOTS,), ((0, 16),), -0.2, 0.2)), 0.2, 2.0)
    sounding_weight = draw_sounding_weight(jax.random.fold_in(key_of[10], 71), 0)
    return {"concentration": concentration, "adjoint_later": adjoint_later, "courant_east": courant_east, "courant_north": courant_north, "diffusivity": diffusivity, "tracer_factor": tracer_factor, "sounding_cell": sounding_cell, "sounding_value": sounding_value, "sounding_precision": sounding_precision, "sounding_weight": sounding_weight}


def solve_column(centre, coupling_down, coupling_up, sources):
    depth = len(centre)
    ratios = []
    sweeps = [[] for member in sources]
    for height in range(depth):
        if height == 0:
            divisor = centre[0]
        else:
            divisor = centre[height] - coupling_down[height] * ratios[height - 1]
        ratios.append(coupling_up[height] / divisor)
        for member in range(len(sources)):
            amount = sources[member][height]
            if height > 0:
                amount = amount + coupling_down[height] * sweeps[member][height - 1]
            sweeps[member].append(amount / divisor)
    results = []
    for member in range(len(sources)):
        column = [None] * depth
        column[depth - 1] = sweeps[member][depth - 1]
        for height in range(depth - 2, -1, -1):
            column[height] = sweeps[member][height] + ratios[height] * column[height + 1]
        results.append(column)
    return results


def column_matrix(below_first, interfaces):
    coupling_down = [below_first] + interfaces[:-1]
    coupling_up = interfaces
    centre = [1.0 + coupling_down[height] + coupling_up[height] for height in range(len(interfaces))]
    return centre, coupling_down, coupling_up


def advect_back(adjoint, east_face, west_face, north_face, south_face):
    east_side = jnp.roll(adjoint, -1, axis=2)
    west_side = jnp.roll(adjoint, 1, axis=2)
    zero_row = jnp.zeros_like(adjoint[..., :1])
    north_side = jnp.concatenate([adjoint[..., 1:], zero_row], axis=3)
    south_side = jnp.concatenate([zero_row, adjoint[..., :-1]], axis=3)
    return (adjoint + jnp.maximum(east_face, 0.0) * (east_side - adjoint)
            + jnp.minimum(west_face, 0.0) * (adjoint - west_side)
            + jnp.maximum(north_face, 0.0) * (north_side - adjoint)
            + jnp.minimum(south_face, 0.0) * (adjoint - south_side))


def reference(concentration, adjoint_later, courant_east, courant_north, diffusivity, tracer_factor, sounding_cell, sounding_value, sounding_precision, sounding_weight):
    slot_tile = (jnp.arange(SLOTS, dtype=jnp.int32) // CAP) % N_TILE
    live = sounding_cell >= 0
    safe_cells = jnp.maximum(sounding_cell, 0)
    flat_index = (slot_tile * (CX * CY) + safe_cells).astype(jnp.int32)
    total = jnp.sum(concentration, axis=0).reshape(LEV, NX * NY)
    picked = jnp.take(total, flat_index, axis=1)
    column_mean = jnp.sum(sounding_weight * picked.T, axis=1)
    misfit = jnp.where(live, sounding_precision * (column_mean - sounding_value), 0.0)
    forcing = jax.ops.segment_sum(sounding_weight * misfit[:, None], flat_index, num_segments=NX * NY)
    adjoint = adjoint_later + forcing.T.reshape(LEV, NX, NY)[None]
    scale_tracer = tracer_factor[:, None, None]
    interfaces = [scale_tracer * diffusivity[height] for height in range(LEV - 1)]
    interfaces.append(jnp.zeros_like(interfaces[0]))
    centre, coupling_down, coupling_up = column_matrix(jnp.zeros_like(interfaces[0]), interfaces)
    west_face = jnp.roll(courant_east, 1, axis=1)
    latitude = lax.broadcasted_iota(jnp.int32, courant_north.shape, 2)
    north_face = jnp.where(latitude == NY - 1, 0.0, courant_north)
    south_face = jnp.concatenate([jnp.zeros_like(north_face[..., :1]), north_face[..., :-1]], axis=2)
    for step_at in range(STEPS):
        solved = solve_column(centre, coupling_down, coupling_up, [[adjoint[:, height] for height in range(LEV)]])[0]
        adjoint = advect_back(jnp.stack(solved, axis=1), courant_east, west_face, north_face, south_face)
    return adjoint
```

```python
import functools

import jax
import jax.numpy as jnp
from jax import lax
from jax.experimental import pallas as pl
from jax.experimental.pallas import tpu as pltpu
from jax.sharding import PartitionSpec as P


LANES = 128
PAIR = 32
HALF = 16
MIB = 1 << 20


def where_am_i():
    return lax.axis_index("band")


def sublane(shape):
    return lax.broadcasted_iota(jnp.int32, shape, len(shape) - 2)


def lane(shape):
    return lax.broadcasted_iota(jnp.int32, shape, len(shape) - 1)


def packed_rows(members, base):
    place = sublane(members[0].shape)
    out = members[0]
    for q in range(1, 4):
        pick = (((place + 2 * q) & 7) >> 1) == (base >> 1)
        out = jnp.where(pick, pltpu.roll(members[q], 8 - 2 * q, 0), out)
    return out


def unpacked_rows(packed, q):
    return packed if q == 0 else pltpu.roll(packed, 2 * q, 0)


def pack_kernel(
    conc,
    adj,
    east,
    north,
    diff,
    cell,
    value,
    precision,
    weight,
    coef,
    coef_one,
    coef_two,
    adj_one,
    adj_two,
    message,
    fields,
):
    tracers, levels, cols, rows = conc.shape
    blocks = cell.shape[0]
    for h in range(3):
        for j in range(blocks):
            fields[h, j, 0:4, :] = weight[4 * h : 4 * h + 4, LANES * j : LANES * (j + 1)]
    for j in range(blocks):
        fields[3, j, 0:1, :] = cell[j : j + 1, :].astype(jnp.float32)
        fields[3, j, 1:2, :] = value[j : j + 1, :]
        fields[3, j, 2:3, :] = precision[j : j + 1, :]
        fields[3, j, 3:4, :] = jnp.zeros((1, LANES), jnp.float32)
    at = lane((4, LANES))
    for h in range(4):
        for j in range(blocks):
            near = pltpu.roll(fields[h, j, 0:4, :], LANES - HALF, 1)
            after = pltpu.roll(fields[h, (j + 1) % blocks, 0:4, :], LANES - HALF, 1)
            fields[h, j, 4:8, :] = jnp.where(at < LANES - HALF, near, after)
    at = lane((8, LANES))
    place = sublane((8, LANES))
    edge = jnp.where(place < 4, float((cols - 2) * rows), float(2 * rows))
    is_cell = ((place & 3) == 0) & (at >= 96)
    for t in range(message.shape[0]):
        j, i = t // 8, t % 8
        parts = []
        for h in range(4):
            if i:
                part = pltpu.roll(fields[h, j], (32 * h - HALF * (i - 1)) % LANES, 1)
            else:
                turn = (32 * h + HALF) % LANES
                before = pltpu.roll(fields[h, (j - 1) % blocks], turn, 1)
                here = pltpu.roll(fields[h, j], turn, 1)
                part = jnp.where((at & 31) < HALF, before, here)
            parts.append(part)
        both = jnp.where(
            at < 64,
            jnp.where(at < 32, parts[0], parts[1]),
            jnp.where(at < 96, parts[2], parts[3]),
        )
        drop = ((at < 112) & (both < edge)) | ((at >= 112) & (both >= edge))
        message[t] = jnp.where(drop & is_cell, -1.0, both)

    band = where_am_i()
    one = jnp.where(band == 0, cols - 2, 0)
    two = jnp.where(band == 0, 0, cols - 2)

    def level(at_level, carry):
        total = conc[0, at_level]
        for tr in range(1, tracers):
            total = total + conc[tr, at_level]
        members = [total, diff[at_level], east[at_level], north[at_level]]
        for q in range(4):
            coef[q, at_level] = members[q]
        coef_one[at_level] = packed_rows(members, one)
        coef_two[at_level] = packed_rows(members, two)
        members = [adj[tr, at_level] for tr in range(tracers)]
        adj_one[at_level] = packed_rows(members, one)
        adj_two[at_level] = packed_rows(members, two)
        return carry

    lax.fori_loop(0, levels, level, 0, unroll=2)


def three_parts(x):
    first = x.astype(jnp.bfloat16)
    rest = x - first.astype(jnp.float32)
    second = rest.astype(jnp.bfloat16)
    third = (rest - second.astype(jnp.float32)).astype(jnp.bfloat16)
    return first, second, third


def exact_dot(x, onehot, dims):
    out = None
    for part in three_parts(x):
        term = lax.dot_general(part, onehot, (dims, ((), ())), preferred_element_type=jnp.float32)
        out = term if out is None else out + term
    return out


def prepare_kernel(
    factor,
    coef_own,
    coef_other,
    edge_own,
    edge_other,
    slots,
    forcing,
    centre,
    east_part,
    west_part,
    north_part,
    south_part,
    inverse,
    lower,
    ratio,
    total,
    diff,
):
    _, band_levels, cols, rows = coef_own.shape
    levels = 2 * band_levels
    tracers = inverse.shape[0]
    band = where_am_i()
    place = sublane((cols, rows))
    at = lane((cols, rows))
    outside = (place >> 1) == jnp.where(band == 0, (cols - 2) >> 1, 0)

    def assemble(coef, edge, first):
        def level(j, carry):
            packed = edge[j]
            t, d, e, n = [
                jnp.where(outside, unpacked_rows(packed, q), coef[q, j]) for q in range(4)
            ]
            n = jnp.where(at == rows - 1, 0.0, n)
            to_east = jnp.maximum(e, 0.0)
            to_west = jnp.minimum(pltpu.roll(e, 1, 0), 0.0)
            to_north = jnp.maximum(n, 0.0)
            to_south = jnp.minimum(pltpu.roll(n, 1, 1), 0.0)
            g = first + j
            total[g] = t
            diff[g] = d
            east_part[g] = to_east
            west_part[g] = -to_west
            north_part[g] = to_north
            south_part[g] = -to_south
            centre[g] = ((1.0 - to_east) + to_west) + (to_south - to_north)
            return carry

        lax.fori_loop(0, band_levels, level, 0, unroll=2)

    assemble(coef_own, edge_own, band * band_levels)
    assemble(coef_other, edge_other, (1 - band) * band_levels)

    zero = jnp.zeros((cols, rows), jnp.float32)

    def factorise(g, carry):
        d = jnp.where(g < levels - 1, diff[g], 0.0)
        out = []
        for tr in range(tracers):
            above, before = carry[tr]
            kappa = factor[tr] * d
            inv = 1.0 / (((1.0 + above) + kappa) - above * before)
            now = kappa * inv
            inverse[tr, g] = inv
            lower[tr, g] = above * inv
            ratio[tr, g] = now
            out.append((kappa, now))
        return tuple(out)

    lax.fori_loop(0, levels, factorise, tuple((zero, zero) for _ in range(tracers)))

    sources = slots.shape[0]
    chunk = min(16, sources)
    wide = chunk * PAIR
    block_at = lane((8, LANES)) >> 5

    def gathered(first, h):
        pieces = []
        for v in range(chunk // 4):
            out = None
            for i in range(4):
                part = slots[first + 4 * v + i]
                turn = (32 * (i - h)) % LANES
                part = pltpu.roll(part, turn, 1) if turn else part
                out = part if out is None else jnp.where(block_at == i, part, out)
            pieces.append(out)
        return jnp.concatenate(pieces, axis=1)

    def soundings(c):
        fields = [gathered(c * chunk, h) for h in range(4)]
        cell = fields[3][0:1].astype(jnp.int32)
        value = fields[3][1:2]
        precision = fields[3][2:3]
        y = cell & (rows - 1)
        x = lax.shift_right_arithmetic(cell, rows.bit_length() - 1)
        onehot = jnp.where(sublane((rows, wide)) == y, 1.0, 0.0).astype(jnp.bfloat16)
        on_column = jnp.where(sublane((cols, wide)) == x, 1.0, 0.0)
        weights = []
        for g in range(levels):
            side, l = g // band_levels, g % band_levels
            weights.append(fields[l // 4][4 * side + l % 4 : 4 * side + l % 4 + 1])
        picked = exact_dot(total[...].reshape(levels * cols, rows), onehot, ((1,), (0,)))
        mean = weights[0] * picked[0:cols]
        for g in range(1, levels):
            mean = mean + weights[g] * picked[g * cols : (g + 1) * cols]
        mean = jnp.sum(mean * on_column, axis=0, keepdims=True)
        misfit = (precision * (mean - value)) * on_column
        spread = jnp.concatenate([weights[g] * misfit for g in range(levels)], axis=0)
        added = exact_dot(spread, onehot, ((1,), (1,)))
        return added.reshape(levels, cols, rows)

    forcing[...] = soundings(0)
    if sources > chunk:

        def more(c, carry):
            forcing[...] += soundings(c)
            return carry

        lax.fori_loop(1, sources // chunk, more, 0)


def solve_kernel(
    adj_own,
    adj_other,
    edge_own,
    edge_other,
    forcing,
    centre,
    east_part,
    west_part,
    north_part,
    south_part,
    inverse,
    lower,
    ratio,
    kept,
    sent,
    state,
):
    tracers, band_levels, cols, rows = adj_own.shape
    levels = 2 * band_levels
    band = where_am_i()
    place = sublane((cols, rows))
    outside = (place >> 1) == jnp.where(band == 0, (cols - 2) >> 1, 0)
    zeros = tuple(jnp.zeros((cols, rows), jnp.float32) for _ in range(tracers))

    def first_sweep(adj, edge, first, carry):
        def level(j, carry):
            g = first + j
            packed = edge[j]
            force = forcing[g]
            out = []
            for tr in range(tracers):
                a = jnp.where(outside, unpacked_rows(packed, tr), adj[tr, j]) + force
                now = a * inverse[tr, g] + lower[tr, g] * carry[tr]
                state[tr, g] = now
                out.append(now)
            return tuple(out)

        return lax.fori_loop(0, band_levels, level, carry, unroll=2)

    @pl.when(band == 0)
    def _():
        carry = first_sweep(adj_own, edge_own, 0, zeros)
        first_sweep(adj_other, edge_other, band_levels, carry)

    @pl.when(band != 0)
    def _():
        carry = first_sweep(adj_other, edge_other, 0, zeros)
        first_sweep(adj_own, edge_own, band_levels, carry)

    def back_and_advect():
        def level(i, carry):
            g = levels - 1 - i
            mid, e, w, n, s = centre[g], east_part[g], west_part[g], north_part[g], south_part[g]
            out = []
            for tr in range(tracers):
                a = state[tr, g] + ratio[tr, g] * carry[tr]
                out.append(a)
                along = e * pltpu.roll(a, cols - 1, 0) + w * pltpu.roll(a, 1, 0)
                across = n * pltpu.roll(a, rows - 1, 1) + s * pltpu.roll(a, 1, 1)
                state[tr, g] = mid * a + (along + across)
            return tuple(out)

        lax.fori_loop(0, levels, level, zeros)

    def forward():
        def level(g, carry):
            out = []
            for tr in range(tracers):
                now = state[tr, g] * inverse[tr, g] + lower[tr, g] * carry[tr]
                state[tr, g] = now
                out.append(now)
            return tuple(out)

        lax.fori_loop(0, levels, level, zeros, unroll=2)

    back_and_advect()
    forward()
    back_and_advect()

    half = band_levels // 2
    mine = (place >> 2) == band
    own_first = band * band_levels
    other_first = (1 - band) * band_levels

    def hand_out(j, carry):
        for tr in range(tracers):
            kept[tr, j] = state[tr, own_first + j]
            kept[tr, j + half] = state[tr, own_first + j + half]
            sent[tr, j] = jnp.where(
                mine,
                state[tr, other_first + j],
                pltpu.roll(state[tr, other_first + j + half], 4, 0),
            )
        return carry

    lax.fori_loop(0, half, hand_out, 0)


def join_kernel(kept, received, out):
    tracers, band_levels, cols, rows = kept.shape
    half = band_levels // 2
    mine = (sublane((cols, rows)) >> 2) == where_am_i()

    def level(j, carry):
        for tr in range(tracers):
            got = received[tr, j]
            out[tr, j] = jnp.where(mine, kept[tr, j], got)
            out[tr, j + half] = jnp.where(mine, kept[tr, j + half], pltpu.roll(got, 4, 0))
        return carry

    lax.fori_loop(0, half, level, 0)


def f32(*shape):
    return jax.ShapeDtypeStruct(shape, jnp.float32)


def call(kernel, outs, scratch, ops, limit, smem=0):
    vmem = pl.BlockSpec(memory_space=pltpu.VMEM)
    scalars = pl.BlockSpec(memory_space=pltpu.SMEM)

    def run(*args):
        moved = sum(4 * a.size for a in args) + sum(4 * o.size for o in outs)
        return pl.pallas_call(
            kernel,
            out_shape=outs,
            in_specs=[scalars] * smem + [vmem] * (len(args) - smem),
            out_specs=[vmem] * len(outs),
            scratch_shapes=scratch,
            compiler_params=pltpu.CompilerParams(vmem_limit_bytes=limit * MIB),
            cost_estimate=pl.CostEstimate(flops=ops, bytes_accessed=moved, transcendentals=0),
        )(*args)

    return run


def per_device(
    tiles,
    concentration,
    adjoint_later,
    courant_east,
    courant_north,
    diffusivity,
    tracer_factor,
    sounding_cell,
    sounding_value,
    sounding_precision,
    sounding_weight,
):
    tracers, band_levels, cols, rows = concentration.shape
    levels = 2 * band_levels
    blocks = sounding_cell.shape[0] // LANES
    field = f32(band_levels, cols, rows)
    deep = f32(levels, cols, rows)
    full = f32(tracers, levels, cols, rows)

    coef, coef_one, coef_two, adj_one, adj_two, message = call(
        pack_kernel,
        [f32(4, band_levels, cols, rows)] + [field] * 4 + [f32(tiles, 8, LANES)],
        [pltpu.VMEM((4, blocks, 8, LANES), jnp.float32)],
        10**6,
        16,
    )(
        concentration,
        adjoint_later,
        courant_east,
        courant_north,
        diffusivity,
        sounding_cell.reshape(blocks, LANES),
        sounding_value.reshape(blocks, LANES),
        sounding_precision.reshape(blocks, LANES),
        sounding_weight.T,
    )

    both = ("tile", "band")
    same = [(2 * t, 2 * ((t + 1) % tiles)) for t in range(tiles)]
    same += [(2 * t + 1, 2 * ((t - 1) % tiles) + 1) for t in range(tiles)]
    cross = [(2 * t + 1, 2 * ((t + 1) % tiles)) for t in range(tiles)]
    cross += [(2 * t, 2 * ((t - 1) % tiles) + 1) for t in range(tiles)]
    swap = [(0, 1), (1, 0)]

    coef_edge_own = lax.ppermute(coef_one, both, same)
    coef_edge_other = lax.ppermute(coef_two, both, cross)
    coef_other = lax.ppermute(coef, "band", swap)
    slots = lax.all_to_all(
        message.reshape(2 * tiles, 4, LANES), both, split_axis=0, concat_axis=0, tiled=True
    ).reshape(tiles, 8, LANES)
    adj_other = lax.ppermute(adjoint_later, "band", swap)
    adj_edge_own = lax.ppermute(adj_one, both, same)
    adj_edge_other = lax.ppermute(adj_two, both, cross)

    ready = call(
        prepare_kernel,
        [deep] * 6 + [full] * 3,
        [pltpu.VMEM((levels, cols, rows), jnp.float32)] * 2,
        10**8,
        32,
        smem=1,
    )(tracer_factor, coef, coef_other, coef_edge_own, coef_edge_other, slots)

    kept, sent = call(
        solve_kernel,
        [f32(tracers, band_levels, cols, rows), f32(tracers, band_levels // 2, cols, rows)],
        [pltpu.VMEM((tracers, levels, cols, rows), jnp.float32)],
        10**7,
        24,
    )(adjoint_later, adj_other, adj_edge_own, adj_edge_other, *ready)
    received = lax.ppermute(sent, "band", swap)
    return call(join_kernel, [f32(tracers, band_levels, cols, rows)], [], 10**5, 8)(kept, received)[0]


def solution(mesh):
    return jax.shard_map(
        functools.partial(per_device, mesh.shape["tile"]),
        mesh=mesh,
        in_specs=(
            P(None, "band", "tile", None),
            P(None, "band", "tile", None),
            P("band", "tile", None),
            P("band", "tile", None),
            P("band", "tile", None),
            P(),
            P("tile"),
            P("tile"),
            P("tile"),
            P("tile", "band"),
        ),
        out_specs=P(None, "band", "tile", None),
        check_vma=False,
    )
```

```python
import functools

import jax
import jax.numpy as jnp
from jax import lax
from jax.experimental import pallas as pl
from jax.experimental.pallas import tpu as pltpu
from jax.sharding import PartitionSpec as P


LANES = 128
PAIR = 32
HALF = 16
MIB = 1 << 20


def where_am_i():
    return lax.axis_index("band")


def sublane(shape):
    return lax.broadcasted_iota(jnp.int32, shape, len(shape) - 2)


def lane(shape):
    return lax.broadcasted_iota(jnp.int32, shape, len(shape) - 1)


def packed_rows(members, base):
    place = sublane(members[0].shape)
    out = members[0]
    for q in range(1, 4):
        pick = (((place + 2 * q) & 7) >> 1) == (base >> 1)
        out = jnp.where(pick, pltpu.roll(members[q], 8 - 2 * q, 0), out)
    return out


def unpacked_rows(packed, q):
    return packed if q == 0 else pltpu.roll(packed, 2 * q, 0)


def pack_kernel(
    conc_at,
    adj_at,
    east_at,
    north_at,
    diff_at,
    cell_at,
    value_at,
    precision_at,
    weight_at,
    block,
    coef_one,
    coef_two,
    adj_one,
    adj_two,
    message,
    conc,
    cell,
    value,
    precision,
    weight,
    fields,
    done,
):
    tracers, levels, cols, rows = conc.shape
    blocks = cell.shape[0]
    moves = [
        (cell_at, cell),
        (value_at, value),
        (precision_at, precision),
        (weight_at, weight),
        (conc_at, conc),
        (diff_at, block.at[1]),
        (east_at, block.at[2]),
        (north_at, block.at[3]),
        (adj_at, block.at[4 : 4 + tracers]),
    ]
    copies = [pltpu.make_async_copy(a, b, done.at[i]) for i, (a, b) in enumerate(moves)]
    for copy in copies:
        copy.start()
    for copy in copies[:4]:
        copy.wait()
    for h in range(3):
        for j in range(blocks):
            fields[h, j, 0:4, :] = weight[4 * h : 4 * h + 4, LANES * j : LANES * (j + 1)]
    for j in range(blocks):
        fields[3, j, 0:1, :] = cell[j : j + 1, :].astype(jnp.float32)
        fields[3, j, 1:2, :] = value[j : j + 1, :]
        fields[3, j, 2:3, :] = precision[j : j + 1, :]
        fields[3, j, 3:4, :] = jnp.zeros((1, LANES), jnp.float32)
    at = lane((4, LANES))
    for h in range(4):
        for j in range(blocks):
            near = pltpu.roll(fields[h, j, 0:4, :], LANES - HALF, 1)
            after = pltpu.roll(fields[h, (j + 1) % blocks, 0:4, :], LANES - HALF, 1)
            fields[h, j, 4:8, :] = jnp.where(at < LANES - HALF, near, after)
    at = lane((8, LANES))
    place = sublane((8, LANES))
    edge = jnp.where(place < 4, float((cols - 2) * rows), float(2 * rows))
    is_cell = ((place & 3) == 0) & (at >= 96)
    for t in range(message.shape[0]):
        j, i = t // 8, t % 8
        parts = []
        for h in range(4):
            if i:
                part = pltpu.roll(fields[h, j], (32 * h - HALF * (i - 1)) % LANES, 1)
            else:
                turn = (32 * h + HALF) % LANES
                before = pltpu.roll(fields[h, (j - 1) % blocks], turn, 1)
                here = pltpu.roll(fields[h, j], turn, 1)
                part = jnp.where((at & 31) < HALF, before, here)
            parts.append(part)
        both = jnp.where(
            at < 64,
            jnp.where(at < 32, parts[0], parts[1]),
            jnp.where(at < 96, parts[2], parts[3]),
        )
        drop = ((at < 112) & (both < edge)) | ((at >= 112) & (both >= edge))
        message[t] = jnp.where(drop & is_cell, -1.0, both)

    band = where_am_i()
    one = jnp.where(band == 0, cols - 2, 0)
    two = jnp.where(band == 0, 0, cols - 2)

    for copy in copies[4:]:
        copy.wait()

    def level(at_level, carry):
        total = conc[0, at_level]
        for tr in range(1, tracers):
            total = total + conc[tr, at_level]
        block[0, at_level] = total
        members = [total] + [block[q, at_level] for q in range(1, 4)]
        coef_one[at_level] = packed_rows(members, one)
        coef_two[at_level] = packed_rows(members, two)
        members = [block[4 + tr, at_level] for tr in range(tracers)]
        adj_one[at_level] = packed_rows(members, one)
        adj_two[at_level] = packed_rows(members, two)
        return carry

    lax.fori_loop(0, levels, level, 0, unroll=2)


def three_parts(x):
    first = x.astype(jnp.bfloat16)
    rest = x - first.astype(jnp.float32)
    second = rest.astype(jnp.bfloat16)
    third = (rest - second.astype(jnp.float32)).astype(jnp.bfloat16)
    return first, second, third


def exact_dot(x, onehot, dims):
    out = None
    for part in three_parts(x):
        term = lax.dot_general(part, onehot, (dims, ((), ())), preferred_element_type=jnp.float32)
        out = term if out is None else out + term
    return out


def prepare_kernel(
    factor,
    coef_own,
    coef_other,
    edge_own,
    edge_other,
    slots,
    forcing,
    centre,
    east_part,
    west_part,
    north_part,
    south_part,
    inverse,
    lower,
    ratio,
    total,
    diff,
):
    band_levels, cols, rows = coef_own.shape[1:]
    levels = 2 * band_levels
    tracers = inverse.shape[0]
    band = where_am_i()
    place = sublane((cols, rows))
    at = lane((cols, rows))
    outside = (place >> 1) == jnp.where(band == 0, (cols - 2) >> 1, 0)

    def assemble(coef, edge, first):
        def level(j, carry):
            packed = edge[j]
            t, d, e, n = [
                jnp.where(outside, unpacked_rows(packed, q), coef[q, j]) for q in range(4)
            ]
            n = jnp.where(at == rows - 1, 0.0, n)
            to_east = jnp.maximum(e, 0.0)
            to_west = jnp.minimum(pltpu.roll(e, 1, 0), 0.0)
            to_north = jnp.maximum(n, 0.0)
            to_south = jnp.minimum(pltpu.roll(n, 1, 1), 0.0)
            g = first + j
            total[g] = t
            diff[g] = d
            east_part[g] = to_east
            west_part[g] = -to_west
            north_part[g] = to_north
            south_part[g] = -to_south
            centre[g] = ((1.0 - to_east) + to_west) + (to_south - to_north)
            return carry

        lax.fori_loop(0, band_levels, level, 0, unroll=2)

    assemble(coef_own, edge_own, band * band_levels)
    assemble(coef_other, edge_other, (1 - band) * band_levels)

    zero = jnp.zeros((cols, rows), jnp.float32)

    def factorise(g, carry):
        d = jnp.where(g < levels - 1, diff[g], 0.0)
        out = []
        for tr in range(tracers):
            above, before = carry[tr]
            kappa = factor[tr] * d
            inv = 1.0 / (((1.0 + above) + kappa) - above * before)
            now = kappa * inv
            inverse[tr, g] = inv
            lower[tr, g] = above * inv
            ratio[tr, g] = now
            out.append((kappa, now))
        return tuple(out)

    lax.fori_loop(0, levels, factorise, tuple((zero, zero) for _ in range(tracers)))

    sources = slots.shape[0]
    chunk = min(16, sources)
    wide = chunk * PAIR
    block_at = lane((8, LANES)) >> 5

    def gathered(first, h):
        pieces = []
        for v in range(chunk // 4):
            out = None
            for i in range(4):
                part = slots[first + 4 * v + i]
                turn = (32 * (i - h)) % LANES
                part = pltpu.roll(part, turn, 1) if turn else part
                out = part if out is None else jnp.where(block_at == i, part, out)
            pieces.append(out)
        return jnp.concatenate(pieces, axis=1)

    def soundings(c):
        fields = [gathered(c * chunk, h) for h in range(4)]
        cell = fields[3][0:1].astype(jnp.int32)
        value = fields[3][1:2]
        precision = fields[3][2:3]
        y = cell & (rows - 1)
        x = lax.shift_right_arithmetic(cell, rows.bit_length() - 1)
        onehot = jnp.where(sublane((rows, wide)) == y, 1.0, 0.0).astype(jnp.bfloat16)
        on_column = jnp.where(sublane((cols, wide)) == x, 1.0, 0.0)
        weights = []
        for g in range(levels):
            side, l = g // band_levels, g % band_levels
            weights.append(fields[l // 4][4 * side + l % 4 : 4 * side + l % 4 + 1])
        picked = exact_dot(total[...].reshape(levels * cols, rows), onehot, ((1,), (0,)))
        mean = weights[0] * picked[0:cols]
        for g in range(1, levels):
            mean = mean + weights[g] * picked[g * cols : (g + 1) * cols]
        mean = jnp.sum(mean * on_column, axis=0, keepdims=True)
        misfit = (precision * (mean - value)) * on_column
        spread = jnp.concatenate([weights[g] * misfit for g in range(levels)], axis=0)
        added = exact_dot(spread, onehot, ((1,), (1,)))
        return added.reshape(levels, cols, rows)

    forcing[...] = soundings(0)
    if sources > chunk:

        def more(c, carry):
            forcing[...] += soundings(c)
            return carry

        lax.fori_loop(1, sources // chunk, more, 0)


def solve_kernel(
    block_own,
    block_other,
    edge_own,
    edge_other,
    forcing,
    centre,
    east_part,
    west_part,
    north_part,
    south_part,
    inverse,
    lower,
    ratio,
    kept,
    sent,
    state,
):
    tracers = kept.shape[0]
    band_levels, cols, rows = block_own.shape[1:]
    levels = 2 * band_levels
    band = where_am_i()
    place = sublane((cols, rows))
    outside = (place >> 1) == jnp.where(band == 0, (cols - 2) >> 1, 0)
    zeros = tuple(jnp.zeros((cols, rows), jnp.float32) for _ in range(tracers))

    def first_sweep(block, edge, first, carry):
        def level(j, carry):
            g = first + j
            packed = edge[j]
            force = forcing[g]
            out = []
            for tr in range(tracers):
                a = jnp.where(outside, unpacked_rows(packed, tr), block[4 + tr, j]) + force
                now = a * inverse[tr, g] + lower[tr, g] * carry[tr]
                state[tr, g] = now
                out.append(now)
            return tuple(out)

        return lax.fori_loop(0, band_levels, level, carry, unroll=2)

    @pl.when(band == 0)
    def _():
        carry = first_sweep(block_own, edge_own, 0, zeros)
        first_sweep(block_other, edge_other, band_levels, carry)

    @pl.when(band != 0)
    def _():
        carry = first_sweep(block_other, edge_other, 0, zeros)
        first_sweep(block_own, edge_own, band_levels, carry)

    def back_and_advect():
        def level(i, carry):
            g = levels - 1 - i
            mid, e, w, n, s = centre[g], east_part[g], west_part[g], north_part[g], south_part[g]
            out = []
            for tr in range(tracers):
                a = state[tr, g] + ratio[tr, g] * carry[tr]
                out.append(a)
                along = e * pltpu.roll(a, cols - 1, 0) + w * pltpu.roll(a, 1, 0)
                across = n * pltpu.roll(a, rows - 1, 1) + s * pltpu.roll(a, 1, 1)
                state[tr, g] = mid * a + (along + across)
            return tuple(out)

        lax.fori_loop(0, levels, level, zeros, unroll=4)

    def forward():
        def level(g, carry):
            out = []
            for tr in range(tracers):
                now = state[tr, g] * inverse[tr, g] + lower[tr, g] * carry[tr]
                state[tr, g] = now
                out.append(now)
            return tuple(out)

        lax.fori_loop(0, levels, level, zeros, unroll=2)

    back_and_advect()
    forward()
    back_and_advect()

    half = band_levels // 2
    mine = (place >> 2) == band
    own_first = band * band_levels
    other_first = (1 - band) * band_levels

    def hand_out(j, carry):
        for tr in range(tracers):
            kept[tr, j] = state[tr, own_first + j]
            kept[tr, j + half] = state[tr, own_first + j + half]
            sent[tr, j] = jnp.where(
                mine,
                state[tr, other_first + j],
                pltpu.roll(state[tr, other_first + j + half], 4, 0),
            )
        return carry

    lax.fori_loop(0, half, hand_out, 0)


def join_kernel(kept, received, out):
    tracers, band_levels, cols, rows = kept.shape
    half = band_levels // 2
    mine = (sublane((cols, rows)) >> 2) == where_am_i()

    def level(j, carry):
        for tr in range(tracers):
            got = received[tr, j]
            out[tr, j] = jnp.where(mine, kept[tr, j], got)
            out[tr, j + half] = jnp.where(mine, kept[tr, j + half], pltpu.roll(got, 4, 0))
        return carry

    lax.fori_loop(0, half, level, 0)


def f32(*shape):
    return jax.ShapeDtypeStruct(shape, jnp.float32)


def call(kernel, outs, scratch, ops, limit, smem=0, space=pltpu.VMEM):
    vmem = pl.BlockSpec(memory_space=pltpu.VMEM)
    scalars = pl.BlockSpec(memory_space=pltpu.SMEM)

    def run(*args):
        moved = sum(4 * a.size for a in args) + sum(4 * o.size for o in outs)
        return pl.pallas_call(
            kernel,
            out_shape=outs,
            in_specs=[scalars] * smem + [pl.BlockSpec(memory_space=space)] * (len(args) - smem),
            out_specs=[vmem] * len(outs),
            scratch_shapes=scratch,
            compiler_params=pltpu.CompilerParams(vmem_limit_bytes=limit * MIB),
            cost_estimate=pl.CostEstimate(flops=ops, bytes_accessed=moved, transcendentals=0),
        )(*args)

    return run


def per_device(
    tiles,
    concentration,
    adjoint_later,
    courant_east,
    courant_north,
    diffusivity,
    tracer_factor,
    sounding_cell,
    sounding_value,
    sounding_precision,
    sounding_weight,
):
    tracers, band_levels, cols, rows = concentration.shape
    levels = 2 * band_levels
    blocks = sounding_cell.shape[0] // LANES
    field = f32(band_levels, cols, rows)
    deep = f32(levels, cols, rows)
    full = f32(tracers, levels, cols, rows)

    block, coef_one, coef_two, adj_one, adj_two, message = call(
        pack_kernel,
        [f32(4 + tracers, band_levels, cols, rows)] + [field] * 4 + [f32(tiles, 8, LANES)],
        [
            pltpu.VMEM((tracers, band_levels, cols, rows), jnp.float32),
            pltpu.VMEM((blocks, LANES), jnp.int32),
            pltpu.VMEM((blocks, LANES), jnp.float32),
            pltpu.VMEM((blocks, LANES), jnp.float32),
            pltpu.VMEM((band_levels, blocks * LANES), jnp.float32),
            pltpu.VMEM((4, blocks, 8, LANES), jnp.float32),
            pltpu.SemaphoreType.DMA((9,)),
        ],
        10**6,
        54,
        space=pltpu.HBM,
    )(
        concentration,
        adjoint_later,
        courant_east,
        courant_north,
        diffusivity,
        sounding_cell.reshape(blocks, LANES),
        sounding_value.reshape(blocks, LANES),
        sounding_precision.reshape(blocks, LANES),
        sounding_weight.T,
    )

    both = ("tile", "band")
    same = [(2 * t, 2 * ((t + 1) % tiles)) for t in range(tiles)]
    same += [(2 * t + 1, 2 * ((t - 1) % tiles) + 1) for t in range(tiles)]
    cross = [(2 * t + 1, 2 * ((t + 1) % tiles)) for t in range(tiles)]
    cross += [(2 * t, 2 * ((t - 1) % tiles) + 1) for t in range(tiles)]
    swap = [(0, 1), (1, 0)]

    coef_edge_own = lax.ppermute(coef_one, both, same)
    coef_edge_other = lax.ppermute(coef_two, both, cross)
    adj_edge_own = lax.ppermute(adj_one, both, same)
    adj_edge_other = lax.ppermute(adj_two, both, cross)
    block_other = lax.ppermute(block, "band", swap)
    slots = lax.all_to_all(
        message.reshape(2 * tiles, 4, LANES), both, split_axis=0, concat_axis=0, tiled=True
    ).reshape(tiles, 8, LANES)

    ready = call(
        prepare_kernel,
        [deep] * 6 + [full] * 3,
        [pltpu.VMEM((levels, cols, rows), jnp.float32)] * 2,
        10**8,
        32,
        smem=1,
    )(tracer_factor, block, block_other, coef_edge_own, coef_edge_other, slots)

    kept, sent = call(
        solve_kernel,
        [f32(tracers, band_levels, cols, rows), f32(tracers, band_levels // 2, cols, rows)],
        [pltpu.VMEM((tracers, levels, cols, rows), jnp.float32)],
        10**7,
        24,
    )(block, block_other, adj_edge_own, adj_edge_other, *ready)
    received = lax.ppermute(sent, "band", swap)
    return call(join_kernel, [f32(tracers, band_levels, cols, rows)], [], 10**5, 8)(kept, received)[0]


def solution(mesh):
    return jax.shard_map(
        functools.partial(per_device, mesh.shape["tile"]),
        mesh=mesh,
        in_specs=(
            P(None, "band", "tile", None),
            P(None, "band", "tile", None),
            P("band", "tile", None),
            P("band", "tile", None),
            P("band", "tile", None),
            P(),
            P("tile"),
            P("tile"),
            P("tile"),
            P("tile", "band"),
        ),
        out_specs=P(None, "band", "tile", None),
        check_vma=False,
    )
```

```python
import functools

import jax
import jax.numpy as jnp
from jax import lax
from jax.experimental import pallas as pl
from jax.experimental.pallas import tpu as pltpu
from jax.sharding import PartitionSpec as P


LANES = 128
PAIR = 32
HALF = 16
MIB = 1 << 20


def where_am_i():
    return lax.axis_index("band")


def sublane(shape):
    return lax.broadcasted_iota(jnp.int32, shape, len(shape) - 2)


def lane(shape):
    return lax.broadcasted_iota(jnp.int32, shape, len(shape) - 1)


def packed_rows(members, base):
    place = sublane(members[0].shape)
    out = members[0]
    for q in range(1, 4):
        pick = (((place + 2 * q) & 7) >> 1) == (base >> 1)
        out = jnp.where(pick, pltpu.roll(members[q], 8 - 2 * q, 0), out)
    return out


def packed_lines(members, columns):
    place = sublane(members[0].shape)
    lines = [members[0]]
    lines += [pltpu.roll(member, q, 0) for q, member in enumerate(members) if q]
    out = []
    for c in columns:
        one = lines[0]
        for q in range(1, len(members)):
            one = jnp.where(((place - c) & 7) == q, lines[q], one)
        out.append(one)
    return out


def turned(tile, by):
    return pltpu.roll(tile, by % 8, 0) if by % 8 else tile


def unpacked_rows(packed, q):
    return packed if q == 0 else pltpu.roll(packed, 2 * q, 0)


def first_kernel(out):
    out[...] = jnp.zeros(out.shape, jnp.float32)


def pack_kernel(
    first,
    conc,
    adj,
    east,
    north,
    diff,
    cell,
    value,
    precision,
    weight,
    block,
    edge_same,
    edge_cross,
    message,
    fields,
    done,
):
    tracers, levels, cols, rows = conc.shape
    blocks = cell.shape[0]
    moves = [
        (diff, block.at[1]),
        (east, block.at[2]),
        (north, block.at[3]),
        (adj, block.at[4 : 4 + tracers]),
    ]
    copies = [pltpu.make_async_copy(a, b, done.at[i]) for i, (a, b) in enumerate(moves)]
    for copy in copies:
        copy.start()
    for h in range(3):
        for j in range(blocks):
            fields[h, j, 0:4, :] = weight[4 * h : 4 * h + 4, LANES * j : LANES * (j + 1)]
    for j in range(blocks):
        fields[3, j, 0:1, :] = cell[j : j + 1, :].astype(jnp.float32)
        fields[3, j, 1:2, :] = value[j : j + 1, :]
        fields[3, j, 2:3, :] = precision[j : j + 1, :]
        fields[3, j, 3:4, :] = jnp.zeros((1, LANES), jnp.float32)
    at = lane((4, LANES))
    for h in range(4):
        for j in range(blocks):
            near = pltpu.roll(fields[h, j, 0:4, :], LANES - HALF, 1)
            after = pltpu.roll(fields[h, (j + 1) % blocks, 0:4, :], LANES - HALF, 1)
            fields[h, j, 4:8, :] = jnp.where(at < LANES - HALF, near, after)
    at = lane((8, LANES))
    place = sublane((8, LANES))
    edge = jnp.where(place < 4, float((cols - 1) * rows), float(rows))
    is_cell = ((place & 3) == 0) & (at >= 96)
    for t in range(message.shape[0]):
        j, i = t // 8, t % 8
        parts = []
        for h in range(4):
            if i:
                part = pltpu.roll(fields[h, j], (32 * h - HALF * (i - 1)) % LANES, 1)
            else:
                turn = (32 * h + HALF) % LANES
                before = pltpu.roll(fields[h, (j - 1) % blocks], turn, 1)
                here = pltpu.roll(fields[h, j], turn, 1)
                part = jnp.where((at & 31) < HALF, before, here)
            parts.append(part)
        both = jnp.where(
            at < 64,
            jnp.where(at < 32, parts[0], parts[1]),
            jnp.where(at < 96, parts[2], parts[3]),
        )
        drop = ((at < 112) & (both < edge)) | ((at >= 112) & (both >= edge))
        message[t] = jnp.where(drop & is_cell, -1.0, both)

    band = where_am_i()
    first = jnp.where(band == 0, cols - 1, 0)
    columns = [first, cols - 1 - first]

    def level(j, carry):
        total = conc[0, j]
        for tr in range(1, tracers):
            total = total + conc[tr, j]
        block[0, j] = total
        members = [total, diff[j], east[j]] + [adj[tr, j] for tr in range(tracers)]
        edge_same[j], edge_cross[j] = packed_lines(members, columns)
        return carry

    lax.fori_loop(0, levels, level, 0, unroll=2)
    for copy in copies:
        copy.wait()


def three_parts(x):
    first = x.astype(jnp.bfloat16)
    rest = x - first.astype(jnp.float32)
    second = rest.astype(jnp.bfloat16)
    third = (rest - second.astype(jnp.float32)).astype(jnp.bfloat16)
    return first, second, third


def exact_dot(x, onehot, dims):
    out = None
    for part in three_parts(x):
        term = lax.dot_general(part, onehot, (dims, ((), ())), preferred_element_type=jnp.float32)
        out = term if out is None else out + term
    return out


def prepare_kernel(
    factor,
    coef_own,
    coef_other,
    edge_own,
    edge_other,
    slots,
    forcing,
    face,
    centre,
    east_part,
    west_part,
    north_part,
    south_part,
    inverse,
    lower,
    ratio,
    total,
    diff,
):
    band_levels, cols, rows = coef_own.shape[1:]
    levels = 2 * band_levels
    tracers = inverse.shape[0]
    band = where_am_i()
    place = sublane((cols, rows))
    at = lane((cols, rows))
    outside = place == jnp.where(band == 0, cols - 1, 0)

    def assemble(coef, edge, first):
        def level(j, carry):
            packed = edge[j]
            t, d, e = [jnp.where(outside, turned(packed, -q), coef[q, j]) for q in range(3)]
            n = jnp.where(at == rows - 1, 0.0, coef[3, j])
            to_east = jnp.maximum(e, 0.0)
            to_west = jnp.minimum(pltpu.roll(e, 1, 0), 0.0)
            to_north = jnp.maximum(n, 0.0)
            to_south = jnp.minimum(pltpu.roll(n, 1, 1), 0.0)
            g = first + j
            total[g] = t
            diff[g] = d
            face[g] = e
            east_part[g] = to_east
            west_part[g] = -to_west
            north_part[g] = to_north
            south_part[g] = -to_south
            centre[g] = ((1.0 - to_east) + to_west) + (to_south - to_north)
            return carry

        lax.fori_loop(0, band_levels, level, 0, unroll=2)

    assemble(coef_own, edge_own, band * band_levels)
    assemble(coef_other, edge_other, (1 - band) * band_levels)

    zero = jnp.zeros((cols, rows), jnp.float32)

    def factorise(g, carry):
        d = jnp.where(g < levels - 1, diff[g], 0.0)
        out = []
        for tr in range(tracers):
            above, before = carry[tr]
            kappa = factor[tr] * d
            inv = 1.0 / (((1.0 + above) + kappa) - above * before)
            now = kappa * inv
            inverse[tr, g] = inv
            lower[tr, g] = above * inv
            ratio[tr, g] = now
            out.append((kappa, now))
        return tuple(out)

    lax.fori_loop(0, levels, factorise, tuple((zero, zero) for _ in range(tracers)))

    sources = slots.shape[0]
    chunk = min(16, sources)
    wide = chunk * PAIR
    block_at = lane((8, LANES)) >> 5

    def gathered(first, h):
        pieces = []
        for v in range(chunk // 4):
            out = None
            for i in range(4):
                part = slots[first + 4 * v + i]
                turn = (32 * (i - h)) % LANES
                part = pltpu.roll(part, turn, 1) if turn else part
                out = part if out is None else jnp.where(block_at == i, part, out)
            pieces.append(out)
        return jnp.concatenate(pieces, axis=1)

    def soundings(c):
        fields = [gathered(c * chunk, h) for h in range(4)]
        cell = fields[3][0:1].astype(jnp.int32)
        value = fields[3][1:2]
        precision = fields[3][2:3]
        y = cell & (rows - 1)
        x = lax.shift_right_arithmetic(cell, rows.bit_length() - 1)
        onehot = jnp.where(sublane((rows, wide)) == y, 1.0, 0.0).astype(jnp.bfloat16)
        on_column = jnp.where(sublane((cols, wide)) == x, 1.0, 0.0)
        weights = []
        for g in range(levels):
            side, l = g // band_levels, g % band_levels
            weights.append(fields[l // 4][4 * side + l % 4 : 4 * side + l % 4 + 1])
        picked = exact_dot(total[...].reshape(levels * cols, rows), onehot, ((1,), (0,)))
        mean = weights[0] * picked[0:cols]
        for g in range(1, levels):
            mean = mean + weights[g] * picked[g * cols : (g + 1) * cols]
        mean = jnp.sum(mean * on_column, axis=0, keepdims=True)
        misfit = (precision * (mean - value)) * on_column
        spread = jnp.concatenate([weights[g] * misfit for g in range(levels)], axis=0)
        added = exact_dot(spread, onehot, ((1,), (1,)))
        return added.reshape(levels, cols, rows)

    forcing[...] = soundings(0)
    if sources > chunk:

        def more(c, carry):
            forcing[...] += soundings(c)
            return carry

        lax.fori_loop(1, sources // chunk, more, 0)


def solve_kernel(
    block_own,
    block_other,
    edge_own,
    edge_other,
    forcing,
    face,
    centre,
    east_part,
    west_part,
    north_part,
    south_part,
    inverse,
    lower,
    ratio,
    kept,
    to_band,
    to_cross,
    to_same,
    state,
):
    tracers = kept.shape[0]
    band_levels, cols, rows = block_own.shape[1:]
    levels = 2 * band_levels
    band = where_am_i()
    place = sublane((cols, rows))
    outside = place == jnp.where(band == 0, cols - 1, 0)
    zeros = tuple(jnp.zeros((cols, rows), jnp.float32) for _ in range(tracers))

    def first_sweep(block, edge, first, carry):
        def level(j, carry):
            g = first + j
            packed = edge[j]
            force = forcing[g]
            out = []
            for tr in range(tracers):
                a = jnp.where(outside, turned(packed, -3 - tr), block[4 + tr, j]) + force
                now = a * inverse[tr, g] + lower[tr, g] * carry[tr]
                state[tr, g] = now
                out.append(now)
            return tuple(out)

        return lax.fori_loop(0, band_levels, level, carry, unroll=2)

    @pl.when(band == 0)
    def _():
        carry = first_sweep(block_own, edge_own, 0, zeros)
        first_sweep(block_other, edge_other, band_levels, carry)

    @pl.when(band != 0)
    def _():
        carry = first_sweep(block_other, edge_other, 0, zeros)
        first_sweep(block_own, edge_own, band_levels, carry)

    def back_and_advect():
        def level(i, carry):
            g = levels - 1 - i
            mid, e, w, n, s = centre[g], east_part[g], west_part[g], north_part[g], south_part[g]
            out = []
            for tr in range(tracers):
                a = state[tr, g] + ratio[tr, g] * carry[tr]
                out.append(a)
                along = e * pltpu.roll(a, cols - 1, 0) + w * pltpu.roll(a, 1, 0)
                across = n * pltpu.roll(a, rows - 1, 1) + s * pltpu.roll(a, 1, 1)
                state[tr, g] = mid * a + (along + across)
            return tuple(out)

        lax.fori_loop(0, levels, level, zeros, unroll=4)

    def forward():
        def level(g, carry):
            out = []
            for tr in range(tracers):
                now = state[tr, g] * inverse[tr, g] + lower[tr, g] * carry[tr]
                state[tr, g] = now
                out.append(now)
            return tuple(out)

        lax.fori_loop(0, levels, level, zeros, unroll=2)

    def back():
        def level(i, carry):
            g = levels - 1 - i
            out = []
            for tr in range(tracers):
                now = state[tr, g] + ratio[tr, g] * carry[tr]
                state[tr, g] = now
                out.append(now)
            return tuple(out)

        lax.fori_loop(0, levels, level, zeros, unroll=4)

    back_and_advect()
    forward()
    back()

    half = band_levels // 2
    own_first = band * band_levels
    other_first = (1 - band) * band_levels
    edge = jnp.where(band == 0, 0, cols - 1)

    def hand_out(j, carry):
        for l in (j, j + half):
            others = [state[tr, other_first + l] for tr in range(tracers)]
            to_band[l] = packed_rows(others, jnp.where(band == 0, 0, cols - 2))
            to_band[band_levels + l] = face[other_first + l]
            for tr in range(tracers):
                kept[tr, l] = state[tr, own_first + l]
        for first, out in ((other_first, to_cross), (own_first, to_same)):
            members = [state[tr, first + l] for l in (j, j + half) for tr in range(tracers)]
            out[j] = packed_lines(members, [edge])[0]
        return carry

    lax.fori_loop(0, half, hand_out, 0)


def finish_kernel(kept, from_band, from_cross, from_same, block, face, out):
    tracers, band_levels, cols, rows = kept.shape
    half = band_levels // 2
    band = where_am_i()
    place = sublane((cols, rows))
    at = lane((cols, rows))
    outside = (place >> 1) == jnp.where(band == 0, (cols - 2) >> 1, 0)
    own_first = band * band_levels

    def pair(j, carry):
        cross, same = from_cross[j], from_same[j]
        westward = jnp.where(band == 0, cross, same)
        eastward = jnp.where(band == 0, same, cross)
        for side in range(2):
            l = j + side * half
            e = block[2, l]
            n = jnp.where(at == rows - 1, 0.0, block[3, l])
            before = jnp.where(band == 0, face[own_first + l], from_band[band_levels + l])
            w = pltpu.roll(jnp.where(place == cols - 1, before, e), 1, 0)
            to_east = jnp.maximum(e, 0.0)
            to_west = jnp.minimum(w, 0.0)
            to_north = jnp.maximum(n, 0.0)
            to_south = jnp.minimum(pltpu.roll(n, 1, 1), 0.0)
            centre = ((1.0 - to_east) + to_west) + (to_south - to_north)
            got = from_band[l]
            for tr in range(tracers):
                q = tr + 4 * side
                a = jnp.where(outside, unpacked_rows(got, tr), kept[tr, l])
                a_east = jnp.where(
                    place == cols - 1, turned(eastward, -1 - q), pltpu.roll(a, cols - 1, 0)
                )
                a_west = jnp.where(place == 0, turned(westward, 1 - q), pltpu.roll(a, 1, 0))
                along = to_east * a_east - to_west * a_west
                across = to_north * pltpu.roll(a, rows - 1, 1) - to_south * pltpu.roll(a, 1, 1)
                out[tr, l] = centre * a + (along + across)
        return carry

    lax.fori_loop(0, half, pair, 0)


def f32(*shape):
    return jax.ShapeDtypeStruct(shape, jnp.float32)


def call(kernel, outs, scratch, ops, limit, smem=0, space=pltpu.VMEM):
    vmem = pl.BlockSpec(memory_space=pltpu.VMEM)
    scalars = pl.BlockSpec(memory_space=pltpu.SMEM)

    def run(*args):
        moved = sum(4 * a.size for a in args) + sum(4 * o.size for o in outs)
        return pl.pallas_call(
            kernel,
            out_shape=outs,
            in_specs=[scalars] * smem + [pl.BlockSpec(memory_space=space)] * (len(args) - smem),
            out_specs=[vmem] * len(outs),
            scratch_shapes=scratch,
            compiler_params=pltpu.CompilerParams(vmem_limit_bytes=limit * MIB),
            cost_estimate=pl.CostEstimate(flops=ops, bytes_accessed=moved, transcendentals=0),
        )(*args)

    return run


def per_device(
    tiles,
    concentration,
    adjoint_later,
    courant_east,
    courant_north,
    diffusivity,
    tracer_factor,
    sounding_cell,
    sounding_value,
    sounding_precision,
    sounding_weight,
):
    tracers, band_levels, cols, rows = concentration.shape
    levels = 2 * band_levels
    blocks = sounding_cell.shape[0] // LANES
    field = f32(band_levels, cols, rows)
    deep = f32(levels, cols, rows)
    full = f32(tracers, levels, cols, rows)

    first = call(first_kernel, [f32(8, LANES)], [], 10**9, 8)()[0]
    block, edge_same, edge_cross, message = call(
        pack_kernel,
        [f32(4 + tracers, band_levels, cols, rows), field, field, f32(tiles, 8, LANES)],
        [pltpu.VMEM((4, blocks, 8, LANES), jnp.float32), pltpu.SemaphoreType.DMA((4,))],
        10**6,
        16,
    )(
        first,
        concentration,
        adjoint_later,
        courant_east,
        courant_north,
        diffusivity,
        sounding_cell.reshape(blocks, LANES),
        sounding_value.reshape(blocks, LANES),
        sounding_precision.reshape(blocks, LANES),
        sounding_weight.T,
    )

    both = ("tile", "band")
    same = [(2 * t, 2 * ((t + 1) % tiles)) for t in range(tiles)]
    same += [(2 * t + 1, 2 * ((t - 1) % tiles) + 1) for t in range(tiles)]
    cross = [(2 * t + 1, 2 * ((t + 1) % tiles)) for t in range(tiles)]
    cross += [(2 * t, 2 * ((t - 1) % tiles) + 1) for t in range(tiles)]
    along = [(2 * t + 1, 2 * ((t + 1) % tiles) + 1) for t in range(tiles)]
    along += [(2 * t, 2 * ((t - 1) % tiles)) for t in range(tiles)]
    swap = [(0, 1), (1, 0)]

    edge_own = lax.ppermute(edge_same, both, same)
    edge_other = lax.ppermute(edge_cross, both, cross)
    block_other = lax.ppermute(block, "band", swap)
    slots = lax.all_to_all(
        message.reshape(2 * tiles, 4, LANES), both, split_axis=0, concat_axis=0, tiled=True
    ).reshape(tiles, 8, LANES)

    forcing, face, *ready = call(
        prepare_kernel,
        [deep] * 7 + [full] * 3,
        [pltpu.VMEM((levels, cols, rows), jnp.float32)] * 2,
        10**8,
        32,
        smem=1,
    )(tracer_factor, block, block_other, edge_own, edge_other, slots)

    part = f32(band_levels // 2, cols, rows)
    kept, to_band, to_cross, to_same = call(
        solve_kernel,
        [f32(tracers, band_levels, cols, rows), deep, part, part],
        [pltpu.VMEM((tracers, levels, cols, rows), jnp.float32)],
        10**7,
        24,
    )(block, block_other, edge_own, edge_other, forcing, face, *ready)
    from_cross = lax.ppermute(to_cross, both, cross)
    from_same = lax.ppermute(to_same, both, along)
    from_band = lax.ppermute(to_band, "band", swap)
    return call(finish_kernel, [f32(tracers, band_levels, cols, rows)], [], 10**6, 16)(
        kept, from_band, from_cross, from_same, block, face
    )[0]


def solution(mesh):
    return jax.shard_map(
        functools.partial(per_device, mesh.shape["tile"]),
        mesh=mesh,
        in_specs=(
            P(None, "band", "tile", None),
            P(None, "band", "tile", None),
            P("band", "tile", None),
            P("band", "tile", None),
            P("band", "tile", None),
            P(),
            P("tile"),
            P("tile"),
            P("tile"),
            P("tile", "band"),
        ),
        out_specs=P(None, "band", "tile", None),
        check_vma=False,
    )
```

```python
import functools

import jax
import jax.numpy as jnp
from jax import lax
from jax.experimental import pallas as pl
from jax.experimental.pallas import tpu as pltpu
from jax.sharding import PartitionSpec as P


LANES = 128
PAIR = 32
HALF = 16
MIB = 1 << 20
GROUP = 2
UNROLL_A = 2
UNROLL_B = 2
UNROLL_C = 2
UNROLL_D = 1


def where_am_i():
    return lax.axis_index("band")


def sublane(shape):
    return lax.broadcasted_iota(jnp.int32, shape, len(shape) - 2)


def lane(shape):
    return lax.broadcasted_iota(jnp.int32, shape, len(shape) - 1)


def packed_rows(members, base):
    place = sublane(members[0].shape)
    out = members[0]
    for q in range(1, 4):
        pick = (((place + 2 * q) & 7) >> 1) == (base >> 1)
        out = jnp.where(pick, pltpu.roll(members[q], 8 - 2 * q, 0), out)
    return out


def packed_lines(members, columns):
    place = sublane(members[0].shape)
    lines = [members[0]]
    lines += [pltpu.roll(member, q, 0) for q, member in enumerate(members) if q]
    out = []
    for c in columns:
        one = lines[0]
        for q in range(1, len(members)):
            one = jnp.where(((place - c) & 7) == q, lines[q], one)
        out.append(one)
    return out


def turned(tile, by):
    return pltpu.roll(tile, by % 8, 0) if by % 8 else tile


def unpacked_rows(packed, q):
    return packed if q == 0 else pltpu.roll(packed, 2 * q, 0)


def first_kernel(out):
    out[...] = jnp.zeros(out.shape, jnp.float32)


def pack_kernel(
    first,
    conc,
    adj,
    east,
    north,
    diff,
    cell,
    value,
    precision,
    weight,
    block,
    edge_same,
    edge_cross,
    message,
    fields,
    done,
):
    tracers, levels, cols, rows = conc.shape
    blocks = cell.shape[0]
    moves = [
        (diff, block.at[1]),
        (east, block.at[2]),
        (north, block.at[3]),
        (adj, block.at[4 : 4 + tracers]),
    ]
    copies = [pltpu.make_async_copy(a, b, done.at[i]) for i, (a, b) in enumerate(moves)]
    for copy in copies:
        copy.start()
    for h in range(3):
        for j in range(blocks):
            fields[h, j, 0:4, :] = weight[4 * h : 4 * h + 4, LANES * j : LANES * (j + 1)]
    for j in range(blocks):
        fields[3, j, 0:1, :] = cell[j : j + 1, :].astype(jnp.float32)
        fields[3, j, 1:2, :] = value[j : j + 1, :]
        fields[3, j, 2:3, :] = precision[j : j + 1, :]
        fields[3, j, 3:4, :] = jnp.zeros((1, LANES), jnp.float32)
    at = lane((4, LANES))
    for h in range(4):
        for j in range(blocks):
            near = pltpu.roll(fields[h, j, 0:4, :], LANES - HALF, 1)
            after = pltpu.roll(fields[h, (j + 1) % blocks, 0:4, :], LANES - HALF, 1)
            fields[h, j, 4:8, :] = jnp.where(at < LANES - HALF, near, after)
    at = lane((8, LANES))
    place = sublane((8, LANES))
    edge = jnp.where(place < 4, float((cols - 1) * rows), float(rows))
    is_cell = ((place & 3) == 0) & (at >= 96)
    for t in range(message.shape[0]):
        j, i = t // 8, t % 8
        parts = []
        for h in range(4):
            if i:
                part = pltpu.roll(fields[h, j], (32 * h - HALF * (i - 1)) % LANES, 1)
            else:
                turn = (32 * h + HALF) % LANES
                before = pltpu.roll(fields[h, (j - 1) % blocks], turn, 1)
                here = pltpu.roll(fields[h, j], turn, 1)
                part = jnp.where((at & 31) < HALF, before, here)
            parts.append(part)
        both = jnp.where(
            at < 64,
            jnp.where(at < 32, parts[0], parts[1]),
            jnp.where(at < 96, parts[2], parts[3]),
        )
        drop = ((at < 112) & (both < edge)) | ((at >= 112) & (both >= edge))
        message[t] = jnp.where(drop & is_cell, -1.0, both)

    band = where_am_i()
    first = jnp.where(band == 0, cols - 1, 0)
    columns = [first, cols - 1 - first]

    def level(j, carry):
        total = conc[0, j]
        for tr in range(1, tracers):
            total = total + conc[tr, j]
        block[0, j] = total
        members = [total, diff[j], east[j]] + [adj[tr, j] for tr in range(tracers)]
        edge_same[j], edge_cross[j] = packed_lines(members, columns)
        return carry

    lax.fori_loop(0, levels, level, 0, unroll=2)
    for copy in copies:
        copy.wait()


def three_parts(x):
    first = x.astype(jnp.bfloat16)
    rest = x - first.astype(jnp.float32)
    second = rest.astype(jnp.bfloat16)
    third = (rest - second.astype(jnp.float32)).astype(jnp.bfloat16)
    return first, second, third


def exact_dot(x, onehot, dims):
    out = None
    for part in three_parts(x):
        term = lax.dot_general(part, onehot, (dims, ((), ())), preferred_element_type=jnp.float32)
        out = term if out is None else out + term
    return out


def add_soundings(slots, total, forcing):
    levels, cols, rows = total.shape
    band_levels = levels // 2
    sources = slots.shape[0]
    chunk = min(16, sources)
    wide = chunk * PAIR
    block_at = lane((8, LANES)) >> 5

    def gathered(first, h):
        pieces = []
        for v in range(chunk // 4):
            out = None
            for i in range(4):
                part = slots[first + 4 * v + i]
                turn = (32 * (i - h)) % LANES
                part = pltpu.roll(part, turn, 1) if turn else part
                out = part if out is None else jnp.where(block_at == i, part, out)
            pieces.append(out)
        return jnp.concatenate(pieces, axis=1)

    def soundings(c):
        fields = [gathered(c * chunk, h) for h in range(4)]
        cell = fields[3][0:1].astype(jnp.int32)
        value = fields[3][1:2]
        precision = fields[3][2:3]
        y = cell & (rows - 1)
        x = lax.shift_right_arithmetic(cell, rows.bit_length() - 1)
        onehot = jnp.where(sublane((rows, wide)) == y, 1.0, 0.0).astype(jnp.bfloat16)
        on_column = jnp.where(sublane((cols, wide)) == x, 1.0, 0.0)
        weights = []
        for g in range(levels):
            side, l = g // band_levels, g % band_levels
            weights.append(fields[l // 4][4 * side + l % 4 : 4 * side + l % 4 + 1])
        picked = exact_dot(total[...].reshape(levels * cols, rows), onehot, ((1,), (0,)))
        mean = weights[0] * picked[0:cols]
        for g in range(1, levels):
            mean = mean + weights[g] * picked[g * cols : (g + 1) * cols]
        mean = jnp.sum(mean * on_column, axis=0, keepdims=True)
        misfit = (precision * (mean - value)) * on_column
        spread = jnp.concatenate([weights[g] * misfit for g in range(levels)], axis=0)
        added = exact_dot(spread, onehot, ((1,), (1,)))
        return added.reshape(levels, cols, rows)

    forcing[...] = soundings(0)
    if sources > chunk:

        def more(c, carry):
            forcing[...] += soundings(c)
            return carry

        lax.fori_loop(1, sources // chunk, more, 0)


def core_kernel(
    factor,
    block_own,
    block_other,
    edge_own,
    edge_other,
    slots,
    kept,
    face,
    to_band,
    to_cross,
    to_same,
    total,
    diff,
    forcing,
    inverse,
    lower,
    ratio,
    middle,
    state,
):
    tracers, count, cols, rows = kept.shape
    levels = 2 * count
    band = where_am_i()
    place = sublane((cols, rows))
    at = lane((cols, rows))
    outside = place == jnp.where(band == 0, cols - 1, 0)
    blocks = (block_own, block_other)
    edges = (edge_own, edge_other)

    def level_of(chain, i):
        up = band == chain
        g = jnp.where(up, i, levels - 1 - i)
        return g, jnp.where(up, i, count - 1 - i)

    def face_of(chain, i):
        return face[i] if chain == 0 else to_band[count + i]

    def assemble(i, carry):
        for chain in range(2):
            g, l = level_of(chain, i)
            packed = edges[chain][l]
            t, d, e = [
                jnp.where(outside, turned(packed, -q), blocks[chain][q, l]) for q in range(3)
            ]
            total[g] = t
            diff[g] = d
            if chain == 0:
                face[i] = e
            else:
                to_band[count + i] = e
        return carry

    lax.fori_loop(0, count, assemble, 0, unroll=UNROLL_A)

    add_soundings(slots, total, forcing)

    def coupling(chain, i):
        return diff[jnp.where(band == chain, i, levels - 2 - i)]

    zero = jnp.zeros((cols, rows), jnp.float32)

    def both(group):
        return [(chain, tr) for chain in range(2) for tr in group]

    def first_sweep(group):
        def level(i, carry):
            out = []
            for chain in range(2):
                g, l = level_of(chain, i)
                inward = coupling(chain, i)
                outward = jnp.where(i > 0, coupling(chain, jnp.maximum(i - 1, 0)), 0.0)
                force = forcing[g]
                packed = edges[chain][l]
                for tr in group:
                    rest, before = carry[len(out)]
                    k_in = factor[tr] * inward
                    k_out = factor[tr] * outward
                    left = 1.0 + k_out * rest
                    inv = 1.0 / (left + k_in)
                    low = k_out * inv
                    a = jnp.where(outside, turned(packed, -3 - tr), blocks[chain][4 + tr, l])
                    now = (a + force) * inv + low * before
                    inverse[chain, tr, i] = inv
                    lower[chain, tr, i] = low
                    ratio[chain, tr, i] = k_in * inv
                    state[chain, tr, i] = now
                    out.append((left * inv, now))
            return tuple(out)

        start = tuple((zero, zero) for _ in both(group))
        ends = lax.fori_loop(0, count, level, start, unroll=UNROLL_B)
        for n, tr in enumerate(group):
            near, far = ends[n][0], ends[n + len(group)][0]
            middle[tr] = 1.0 / (near + ratio[0, tr, count - 1] * far)

    def meet(group):
        ends = []
        for chain, tr in both(group):
            mine, others = state[chain, tr, count - 1], state[1 - chain, tr, count - 1]
            ends.append((mine + ratio[chain, tr, count - 1] * others) * middle[tr])
        return tuple(ends)

    def forward(group):
        def level(i, carry):
            out = []
            for chain, tr in both(group):
                now = (
                    state[chain, tr, i] * inverse[chain, tr, i]
                    + lower[chain, tr, i] * carry[len(out)]
                )
                state[chain, tr, i] = now
                out.append(now)
            return tuple(out)

        lax.fori_loop(0, count, level, tuple(zero for _ in both(group)), unroll=UNROLL_C)

    def backward(group):
        ends = meet(group)
        for n, (chain, tr) in enumerate(both(group)):
            state[chain, tr, count - 1] = ends[n]

        def level(step, carry):
            i = count - 2 - step
            out = []
            for chain, tr in both(group):
                now = state[chain, tr, i] + ratio[chain, tr, i] * carry[len(out)]
                state[chain, tr, i] = now
                out.append(now)
            return tuple(out)

        lax.fori_loop(0, count - 1, level, ends, unroll=UNROLL_C)

    def advect(i, carry):
        for chain in range(2):
            _, l = level_of(chain, i)
            e = face_of(chain, i)
            n = jnp.where(at == rows - 1, 0.0, blocks[chain][3, l])
            to_east = jnp.maximum(e, 0.0)
            to_west = jnp.minimum(pltpu.roll(e, 1, 0), 0.0)
            to_north = jnp.maximum(n, 0.0)
            to_south = jnp.minimum(pltpu.roll(n, 1, 1), 0.0)
            centre = ((1.0 - to_east) + to_west) + (to_south - to_north)
            for tr in range(tracers):
                a = state[chain, tr, i]
                along = to_east * pltpu.roll(a, cols - 1, 0) - to_west * pltpu.roll(a, 1, 0)
                across = to_north * pltpu.roll(a, rows - 1, 1) - to_south * pltpu.roll(a, 1, 1)
                state[chain, tr, i] = centre * a + (along + across)
        return carry

    groups = [range(tr, min(tr + GROUP, tracers)) for tr in range(0, tracers, GROUP)]
    for group in groups:
        first_sweep(group)
    for group in groups:
        backward(group)
    lax.fori_loop(0, count, advect, 0, unroll=UNROLL_D)
    for group in groups:
        forward(group)
    for group in groups:
        backward(group)

    edge = jnp.where(band == 0, 0, cols - 1)

    def hand_out(j, carry):
        for i in (2 * j, 2 * j + 1):
            to_band[i] = packed_rows(
                [state[1, tr, i] for tr in range(tracers)], jnp.where(band == 0, 0, cols - 2)
            )
            for tr in range(tracers):
                kept[tr, i] = state[0, tr, i]
        for chain, out in ((1, to_cross), (0, to_same)):
            members = [state[chain, tr, i] for i in (2 * j, 2 * j + 1) for tr in range(tracers)]
            out[j] = packed_lines(members, [edge])[0]
        return carry

    lax.fori_loop(0, count // 2, hand_out, 0)


def finish_kernel(kept, from_band, block, face, inner, sides):
    tracers, count, cols, rows = kept.shape
    band = where_am_i()
    place = sublane((cols, rows))
    at = lane((cols, rows))
    outside = (place >> 1) == jnp.where(band == 0, (cols - 2) >> 1, 0)

    def level(i, carry):
        l = jnp.where(band == 0, i, count - 1 - i)
        e = block[2, l]
        n = jnp.where(at == rows - 1, 0.0, block[3, l])
        before = jnp.where(band == 0, face[i], from_band[count + i])
        w = pltpu.roll(jnp.where(place == cols - 1, before, e), 1, 0)
        to_east = jnp.maximum(e, 0.0)
        to_west = jnp.minimum(w, 0.0)
        to_north = jnp.maximum(n, 0.0)
        to_south = jnp.minimum(pltpu.roll(n, 1, 1), 0.0)
        centre = ((1.0 - to_east) + to_west) + (to_south - to_north)
        sides[i] = jnp.where(
            place == cols - 1, to_east, jnp.where(place == 0, -to_west, 0.0)
        )
        to_east = jnp.where(place == cols - 1, 0.0, to_east)
        to_west = jnp.where(place == 0, 0.0, to_west)
        got = from_band[i]
        for tr in range(tracers):
            a = jnp.where(outside, unpacked_rows(got, tr), kept[tr, i])
            along = to_east * pltpu.roll(a, cols - 1, 0) - to_west * pltpu.roll(a, 1, 0)
            across = to_north * pltpu.roll(a, rows - 1, 1) - to_south * pltpu.roll(a, 1, 1)
            inner[tr, l] = centre * a + (along + across)
        return carry

    lax.fori_loop(0, count, level, 0, unroll=2)


def border_kernel(inner, sides, from_cross, from_same, out):
    tracers, count, cols, rows = inner.shape
    band = where_am_i()
    place = sublane((cols, rows))

    def pair(j, carry):
        cross, same = from_cross[j], from_same[j]
        westward = jnp.where(band == 0, cross, same)
        eastward = jnp.where(band == 0, same, cross)
        for side in range(2):
            i = 2 * j + side
            l = jnp.where(band == 0, i, count - 1 - i)
            for tr in range(tracers):
                q = tr + 4 * side
                beyond = jnp.where(place == 0, turned(westward, 1 - q), turned(eastward, -1 - q))
                out[tr, l] = inner[tr, l] + sides[i] * beyond
        return carry

    lax.fori_loop(0, count // 2, pair, 0, unroll=2)


def f32(*shape):
    return jax.ShapeDtypeStruct(shape, jnp.float32)


def call(kernel, outs, scratch, ops, limit, smem=0, space=pltpu.VMEM):
    vmem = pl.BlockSpec(memory_space=pltpu.VMEM)
    scalars = pl.BlockSpec(memory_space=pltpu.SMEM)

    def run(*args):
        moved = sum(4 * a.size for a in args) + sum(4 * o.size for o in outs)
        return pl.pallas_call(
            kernel,
            out_shape=outs,
            in_specs=[scalars] * smem + [pl.BlockSpec(memory_space=space)] * (len(args) - smem),
            out_specs=[vmem] * len(outs),
            scratch_shapes=scratch,
            compiler_params=pltpu.CompilerParams(vmem_limit_bytes=limit * MIB),
            cost_estimate=pl.CostEstimate(flops=ops, bytes_accessed=moved, transcendentals=0),
        )(*args)

    return run


def per_device(
    tiles,
    concentration,
    adjoint_later,
    courant_east,
    courant_north,
    diffusivity,
    tracer_factor,
    sounding_cell,
    sounding_value,
    sounding_precision,
    sounding_weight,
):
    tracers, band_levels, cols, rows = concentration.shape
    levels = 2 * band_levels
    blocks = sounding_cell.shape[0] // LANES
    field = f32(band_levels, cols, rows)
    deep = f32(levels, cols, rows)

    first = call(first_kernel, [f32(8, LANES)], [], 10**9, 8)()[0]
    block, edge_same, edge_cross, message = call(
        pack_kernel,
        [f32(4 + tracers, band_levels, cols, rows), field, field, f32(tiles, 8, LANES)],
        [pltpu.VMEM((4, blocks, 8, LANES), jnp.float32), pltpu.SemaphoreType.DMA((4,))],
        10**6,
        16,
    )(
        first,
        concentration,
        adjoint_later,
        courant_east,
        courant_north,
        diffusivity,
        sounding_cell.reshape(blocks, LANES),
        sounding_value.reshape(blocks, LANES),
        sounding_precision.reshape(blocks, LANES),
        sounding_weight.T,
    )

    both = ("tile", "band")
    same = [(2 * t, 2 * ((t + 1) % tiles)) for t in range(tiles)]
    same += [(2 * t + 1, 2 * ((t - 1) % tiles) + 1) for t in range(tiles)]
    cross = [(2 * t + 1, 2 * ((t + 1) % tiles)) for t in range(tiles)]
    cross += [(2 * t, 2 * ((t - 1) % tiles) + 1) for t in range(tiles)]
    along = [(2 * t + 1, 2 * ((t + 1) % tiles) + 1) for t in range(tiles)]
    along += [(2 * t, 2 * ((t - 1) % tiles)) for t in range(tiles)]
    swap = [(0, 1), (1, 0)]

    edge_own = lax.ppermute(edge_same, both, same)
    edge_other = lax.ppermute(edge_cross, both, cross)
    block_other = lax.ppermute(block, "band", swap)
    slots = lax.all_to_all(
        message.reshape(2 * tiles, 4, LANES), both, split_axis=0, concat_axis=0, tiled=True
    ).reshape(tiles, 8, LANES)

    part = f32(band_levels // 2, cols, rows)
    whole = f32(tracers, band_levels, cols, rows)
    chains = pltpu.VMEM((2, tracers, band_levels, cols, rows), jnp.float32)
    kept, face, to_band, to_cross, to_same = call(
        core_kernel,
        [whole, field, deep, part, part],
        [pltpu.VMEM((levels, cols, rows), jnp.float32)] * 3
        + [chains] * 3
        + [pltpu.VMEM((tracers, cols, rows), jnp.float32), chains],
        10**8,
        32,
        smem=1,
    )(tracer_factor, block, block_other, edge_own, edge_other, slots)
    from_cross = lax.ppermute(to_cross, both, cross)
    from_same = lax.ppermute(to_same, both, along)
    from_band = lax.ppermute(to_band, "band", swap)
    inner, sides = call(finish_kernel, [whole, field], [], 10**7, 16)(
        kept, from_band, block, face
    )
    return call(border_kernel, [whole], [], 10**6, 16)(inner, sides, from_cross, from_same)[0]


def solution(mesh):
    return jax.shard_map(
        functools.partial(per_device, mesh.shape["tile"]),
        mesh=mesh,
        in_specs=(
            P(None, "band", "tile", None),
            P(None, "band", "tile", None),
            P("band", "tile", None),
            P("band", "tile", None),
            P("band", "tile", None),
            P(),
            P("tile"),
            P("tile"),
            P("tile"),
            P("tile", "band"),
        ),
        out_specs=P(None, "band", "tile", None),
        check_vma=False,
    )
```

```python
import functools

import jax
import jax.numpy as jnp
from jax import lax
from jax.experimental import pallas as pl
from jax.experimental.pallas import tpu as pltpu
from jax.sharding import PartitionSpec as P


LANES = 128
PAIR = 32
HALF = 16
MIB = 1 << 20
GROUP = 4
UNROLL_A = 2
UNROLL_B = 4
UNROLL_C = 2
UNROLL_D = 6


def where_am_i():
    return lax.axis_index("band")


def sublane(shape):
    return lax.broadcasted_iota(jnp.int32, shape, len(shape) - 2)


def lane(shape):
    return lax.broadcasted_iota(jnp.int32, shape, len(shape) - 1)


def packed_rows(members, base):
    place = sublane(members[0].shape)
    out = members[0]
    for q in range(1, 4):
        pick = (((place + 2 * q) & 7) >> 1) == (base >> 1)
        out = jnp.where(pick, pltpu.roll(members[q], 8 - 2 * q, 0), out)
    return out


def packed_lines(members, columns):
    place = sublane(members[0].shape)
    lines = [members[0]]
    lines += [pltpu.roll(member, q, 0) for q, member in enumerate(members) if q]
    out = []
    for c in columns:
        one = lines[0]
        for q in range(1, len(members)):
            one = jnp.where(((place - c) & 7) == q, lines[q], one)
        out.append(one)
    return out


def turned(tile, by):
    return pltpu.roll(tile, by % 8, 0) if by % 8 else tile


def unpacked_rows(packed, q):
    return packed if q == 0 else pltpu.roll(packed, 2 * q, 0)


def first_kernel(out):
    out[...] = jnp.zeros(out.shape, jnp.float32)


def pack_kernel(
    first,
    conc,
    adj,
    east,
    north,
    diff,
    cell,
    value,
    precision,
    weight,
    block,
    edge_same,
    edge_cross,
    message,
    fields,
    done,
):
    tracers, levels, cols, rows = conc.shape
    blocks = cell.shape[0]
    moves = [
        (diff, block.at[1]),
        (east, block.at[2]),
        (north, block.at[3]),
        (adj, block.at[4 : 4 + tracers]),
    ]
    copies = [pltpu.make_async_copy(a, b, done.at[i]) for i, (a, b) in enumerate(moves)]
    for copy in copies:
        copy.start()
    for h in range(3):
        for j in range(blocks):
            fields[h, j, 0:4, :] = weight[4 * h : 4 * h + 4, LANES * j : LANES * (j + 1)]
    for j in range(blocks):
        fields[3, j, 0:1, :] = cell[j : j + 1, :].astype(jnp.float32)
        fields[3, j, 1:2, :] = value[j : j + 1, :]
        fields[3, j, 2:3, :] = precision[j : j + 1, :]
        fields[3, j, 3:4, :] = jnp.zeros((1, LANES), jnp.float32)
    at = lane((4, LANES))
    for h in range(4):
        for j in range(blocks):
            near = pltpu.roll(fields[h, j, 0:4, :], LANES - HALF, 1)
            after = pltpu.roll(fields[h, (j + 1) % blocks, 0:4, :], LANES - HALF, 1)
            fields[h, j, 4:8, :] = jnp.where(at < LANES - HALF, near, after)
    at = lane((8, LANES))
    place = sublane((8, LANES))
    edge = jnp.where(place < 4, float((cols - 1) * rows), float(rows))
    is_cell = ((place & 3) == 0) & (at >= 96)
    for t in range(message.shape[0]):
        j, i = t // 8, t % 8
        parts = []
        for h in range(4):
            if i:
                part = pltpu.roll(fields[h, j], (32 * h - HALF * (i - 1)) % LANES, 1)
            else:
                turn = (32 * h + HALF) % LANES
                before = pltpu.roll(fields[h, (j - 1) % blocks], turn, 1)
                here = pltpu.roll(fields[h, j], turn, 1)
                part = jnp.where((at & 31) < HALF, before, here)
            parts.append(part)
        both = jnp.where(
            at < 64,
            jnp.where(at < 32, parts[0], parts[1]),
            jnp.where(at < 96, parts[2], parts[3]),
        )
        drop = ((at < 112) & (both < edge)) | ((at >= 112) & (both >= edge))
        message[t] = jnp.where(drop & is_cell, -1.0, both)

    band = where_am_i()
    first = jnp.where(band == 0, cols - 1, 0)
    columns = [first, cols - 1 - first]

    def level(j, carry):
        total = conc[0, j]
        for tr in range(1, tracers):
            total = total + conc[tr, j]
        block[0, j] = total
        members = [total, diff[j], east[j]] + [adj[tr, j] for tr in range(tracers)]
        edge_same[j], edge_cross[j] = packed_lines(members, columns)
        return carry

    lax.fori_loop(0, levels, level, 0, unroll=2)
    for copy in copies:
        copy.wait()


def two_parts(x):
    first = x.astype(jnp.bfloat16)
    rest = x - first.astype(jnp.float32)
    second = rest.astype(jnp.bfloat16)
    return first, second


def onehot_dot(x, onehot, dims):
    out = None
    for part in two_parts(x):
        term = lax.dot_general(part, onehot, (dims, ((), ())), preferred_element_type=jnp.float32)
        out = term if out is None else out + term
    return out


def add_soundings(slots, total, forcing):
    levels, cols, rows = total.shape
    band_levels = levels // 2
    sources = slots.shape[0]
    chunk = min(16, sources)
    wide = chunk * PAIR
    block_at = lane((8, LANES)) >> 5

    def gathered(first, h):
        pieces = []
        for v in range(chunk // 4):
            out = None
            for i in range(4):
                part = slots[first + 4 * v + i]
                turn = (32 * (i - h)) % LANES
                part = pltpu.roll(part, turn, 1) if turn else part
                out = part if out is None else jnp.where(block_at == i, part, out)
            pieces.append(out)
        return jnp.concatenate(pieces, axis=1)

    def soundings(c):
        fields = [gathered(c * chunk, h) for h in range(4)]
        cell = fields[3][0:1].astype(jnp.int32)
        value = fields[3][1:2]
        precision = fields[3][2:3]
        y = cell & (rows - 1)
        x = lax.shift_right_arithmetic(cell, rows.bit_length() - 1)
        onehot = jnp.where(sublane((rows, wide)) == y, 1.0, 0.0).astype(jnp.bfloat16)
        on_column = jnp.where(sublane((cols, wide)) == x, 1.0, 0.0)
        weights = []
        for g in range(levels):
            side, l = g // band_levels, g % band_levels
            weights.append(fields[l // 4][4 * side + l % 4 : 4 * side + l % 4 + 1])
        picked = onehot_dot(total[...].reshape(levels * cols, rows), onehot, ((1,), (0,)))
        mean = weights[0] * picked[0:cols]
        for g in range(1, levels):
            mean = mean + weights[g] * picked[g * cols : (g + 1) * cols]
        mean = jnp.sum(mean * on_column, axis=0, keepdims=True)
        misfit = (precision * (mean - value)) * on_column
        spread = jnp.concatenate([weights[g] * misfit for g in range(levels)], axis=0)
        added = onehot_dot(spread, onehot, ((1,), (1,)))
        return added.reshape(levels, cols, rows)

    forcing[...] = soundings(0)
    if sources > chunk:

        def more(c, carry):
            forcing[...] += soundings(c)
            return carry

        lax.fori_loop(1, sources // chunk, more, 0)


def core_kernel(
    factor,
    block_own,
    block_other,
    edge_own,
    edge_other,
    slots,
    kept,
    face,
    to_band,
    to_cross,
    to_same,
    total,
    diff,
    forcing,
    inverse,
    lower,
    ratio,
    middle,
    state,
):
    tracers, count, cols, rows = kept.shape
    levels = 2 * count
    band = where_am_i()
    place = sublane((cols, rows))
    at = lane((cols, rows))
    outside = place == jnp.where(band == 0, cols - 1, 0)
    blocks = (block_own, block_other)
    edges = (edge_own, edge_other)

    def level_of(chain, i):
        up = band == chain
        g = jnp.where(up, i, levels - 1 - i)
        return g, jnp.where(up, i, count - 1 - i)

    def face_of(chain, i):
        return face[i] if chain == 0 else to_band[count + i]

    def assemble(i, carry):
        for chain in range(2):
            g, l = level_of(chain, i)
            packed = edges[chain][l]
            t, d, e = [
                jnp.where(outside, turned(packed, -q), blocks[chain][q, l]) for q in range(3)
            ]
            total[g] = t
            diff[g] = d
            if chain == 0:
                face[i] = e
            else:
                to_band[count + i] = e
        return carry

    lax.fori_loop(0, count, assemble, 0, unroll=UNROLL_A)

    add_soundings(slots, total, forcing)

    def coupling(chain, i):
        return diff[jnp.where(band == chain, i, levels - 2 - i)]

    zero = jnp.zeros((cols, rows), jnp.float32)

    def both(group):
        return [(chain, tr) for chain in range(2) for tr in group]

    def first_sweep(group):
        def level(i, carry):
            out = []
            for chain in range(2):
                g, l = level_of(chain, i)
                inward = coupling(chain, i)
                outward = jnp.where(i > 0, coupling(chain, jnp.maximum(i - 1, 0)), 0.0)
                force = forcing[g]
                packed = edges[chain][l]
                for tr in group:
                    rest, before = carry[len(out)]
                    k_in = factor[tr] * inward
                    k_out = factor[tr] * outward
                    left = 1.0 + k_out * rest
                    inv = 1.0 / (left + k_in)
                    low = k_out * inv
                    a = jnp.where(outside, turned(packed, -3 - tr), blocks[chain][4 + tr, l])
                    now = (a + force) * inv + low * before
                    inverse[chain, tr, i] = inv
                    lower[chain, tr, i] = low
                    ratio[chain, tr, i] = k_in * inv
                    state[chain, tr, i] = now
                    out.append((left * inv, now))
            return tuple(out)

        start = tuple((zero, zero) for _ in both(group))
        ends = lax.fori_loop(0, count, level, start, unroll=UNROLL_B)
        for n, tr in enumerate(group):
            near, far = ends[n][0], ends[n + len(group)][0]
            middle[tr] = 1.0 / (near + ratio[0, tr, count - 1] * far)

    def meet(group):
        ends = []
        for chain, tr in both(group):
            mine, others = state[chain, tr, count - 1], state[1 - chain, tr, count - 1]
            ends.append((mine + ratio[chain, tr, count - 1] * others) * middle[tr])
        return tuple(ends)

    def forward(group):
        def level(i, carry):
            out = []
            for chain, tr in both(group):
                now = (
                    state[chain, tr, i] * inverse[chain, tr, i]
                    + lower[chain, tr, i] * carry[len(out)]
                )
                state[chain, tr, i] = now
                out.append(now)
            return tuple(out)

        lax.fori_loop(0, count, level, tuple(zero for _ in both(group)), unroll=UNROLL_C)

    def backward(group):
        ends = meet(group)
        for n, (chain, tr) in enumerate(both(group)):
            state[chain, tr, count - 1] = ends[n]

        def level(step, carry):
            i = count - 2 - step
            out = []
            for chain, tr in both(group):
                now = state[chain, tr, i] + ratio[chain, tr, i] * carry[len(out)]
                state[chain, tr, i] = now
                out.append(now)
            return tuple(out)

        lax.fori_loop(0, count - 1, level, ends, unroll=UNROLL_C)

    def advect(i, carry):
        for chain in range(2):
            _, l = level_of(chain, i)
            e = face_of(chain, i)
            n = jnp.where(at == rows - 1, 0.0, blocks[chain][3, l])
            to_east = jnp.maximum(e, 0.0)
            to_west = jnp.minimum(pltpu.roll(e, 1, 0), 0.0)
            to_north = jnp.maximum(n, 0.0)
            to_south = jnp.minimum(pltpu.roll(n, 1, 1), 0.0)
            centre = ((1.0 - to_east) + to_west) + (to_south - to_north)
            for tr in range(tracers):
                a = state[chain, tr, i]
                along = to_east * pltpu.roll(a, cols - 1, 0) - to_west * pltpu.roll(a, 1, 0)
                across = to_north * pltpu.roll(a, rows - 1, 1) - to_south * pltpu.roll(a, 1, 1)
                state[chain, tr, i] = centre * a + (along + across)
        return carry

    groups = [range(tr, min(tr + GROUP, tracers)) for tr in range(0, tracers, GROUP)]
    for group in groups:
        first_sweep(group)
    for group in groups:
        backward(group)
    lax.fori_loop(0, count, advect, 0, unroll=UNROLL_D)
    for group in groups:
        forward(group)
    for group in groups:
        backward(group)

    edge = jnp.where(band == 0, 0, cols - 1)

    def hand_out(j, carry):
        for i in (2 * j, 2 * j + 1):
            to_band[i] = packed_rows(
                [state[1, tr, i] for tr in range(tracers)], jnp.where(band == 0, 0, cols - 2)
            )
            for tr in range(tracers):
                kept[tr, i] = state[0, tr, i]
        for chain, out in ((1, to_cross), (0, to_same)):
            members = [state[chain, tr, i] for i in (2 * j, 2 * j + 1) for tr in range(tracers)]
            out[j] = packed_lines(members, [edge])[0]
        return carry

    lax.fori_loop(0, count // 2, hand_out, 0)


def finish_kernel(kept, from_band, block, face, inner, sides):
    tracers, count, cols, rows = kept.shape
    band = where_am_i()
    place = sublane((cols, rows))
    at = lane((cols, rows))
    outside = (place >> 1) == jnp.where(band == 0, (cols - 2) >> 1, 0)

    def level(i, carry):
        l = jnp.where(band == 0, i, count - 1 - i)
        e = block[2, l]
        n = jnp.where(at == rows - 1, 0.0, block[3, l])
        before = jnp.where(band == 0, face[i], from_band[count + i])
        w = pltpu.roll(jnp.where(place == cols - 1, before, e), 1, 0)
        to_east = jnp.maximum(e, 0.0)
        to_west = jnp.minimum(w, 0.0)
        to_north = jnp.maximum(n, 0.0)
        to_south = jnp.minimum(pltpu.roll(n, 1, 1), 0.0)
        centre = ((1.0 - to_east) + to_west) + (to_south - to_north)
        sides[i] = jnp.where(
            place == cols - 1, to_east, jnp.where(place == 0, -to_west, 0.0)
        )
        to_east = jnp.where(place == cols - 1, 0.0, to_east)
        to_west = jnp.where(place == 0, 0.0, to_west)
        got = from_band[i]
        for tr in range(tracers):
            a = jnp.where(outside, unpacked_rows(got, tr), kept[tr, i])
            along = to_east * pltpu.roll(a, cols - 1, 0) - to_west * pltpu.roll(a, 1, 0)
            across = to_north * pltpu.roll(a, rows - 1, 1) - to_south * pltpu.roll(a, 1, 1)
            inner[tr, l] = centre * a + (along + across)
        return carry

    lax.fori_loop(0, count, level, 0, unroll=2)


def border_kernel(inner, sides, from_cross, from_same, out):
    tracers, count, cols, rows = inner.shape
    band = where_am_i()
    place = sublane((cols, rows))

    def pair(j, carry):
        cross, same = from_cross[j], from_same[j]
        westward = jnp.where(band == 0, cross, same)
        eastward = jnp.where(band == 0, same, cross)
        for side in range(2):
            i = 2 * j + side
            l = jnp.where(band == 0, i, count - 1 - i)
            for tr in range(tracers):
                q = tr + 4 * side
                beyond = jnp.where(place == 0, turned(westward, 1 - q), turned(eastward, -1 - q))
                out[tr, l] = inner[tr, l] + sides[i] * beyond
        return carry

    lax.fori_loop(0, count // 2, pair, 0, unroll=2)


def f32(*shape):
    return jax.ShapeDtypeStruct(shape, jnp.float32)


def call(kernel, outs, scratch, ops, limit, smem=0, space=pltpu.VMEM):
    vmem = pl.BlockSpec(memory_space=pltpu.VMEM)
    scalars = pl.BlockSpec(memory_space=pltpu.SMEM)

    def run(*args):
        moved = sum(4 * a.size for a in args) + sum(4 * o.size for o in outs)
        return pl.pallas_call(
            kernel,
            out_shape=outs,
            in_specs=[scalars] * smem + [pl.BlockSpec(memory_space=space)] * (len(args) - smem),
            out_specs=[vmem] * len(outs),
            scratch_shapes=scratch,
            compiler_params=pltpu.CompilerParams(vmem_limit_bytes=limit * MIB),
            cost_estimate=pl.CostEstimate(flops=ops, bytes_accessed=moved, transcendentals=0),
        )(*args)

    return run


def per_device(
    tiles,
    concentration,
    adjoint_later,
    courant_east,
    courant_north,
    diffusivity,
    tracer_factor,
    sounding_cell,
    sounding_value,
    sounding_precision,
    sounding_weight,
):
    tracers, band_levels, cols, rows = concentration.shape
    levels = 2 * band_levels
    blocks = sounding_cell.shape[0] // LANES
    field = f32(band_levels, cols, rows)
    deep = f32(levels, cols, rows)

    first = call(first_kernel, [f32(8, LANES)], [], 10**9, 8)()[0]
    block, edge_same, edge_cross, message = call(
        pack_kernel,
        [f32(4 + tracers, band_levels, cols, rows), field, field, f32(tiles, 8, LANES)],
        [pltpu.VMEM((4, blocks, 8, LANES), jnp.float32), pltpu.SemaphoreType.DMA((4,))],
        10**6,
        16,
    )(
        first,
        concentration,
        adjoint_later,
        courant_east,
        courant_north,
        diffusivity,
        sounding_cell.reshape(blocks, LANES),
        sounding_value.reshape(blocks, LANES),
        sounding_precision.reshape(blocks, LANES),
        sounding_weight.T,
    )

    both = ("tile", "band")
    same = [(2 * t, 2 * ((t + 1) % tiles)) for t in range(tiles)]
    same += [(2 * t + 1, 2 * ((t - 1) % tiles) + 1) for t in range(tiles)]
    cross = [(2 * t + 1, 2 * ((t + 1) % tiles)) for t in range(tiles)]
    cross += [(2 * t, 2 * ((t - 1) % tiles) + 1) for t in range(tiles)]
    along = [(2 * t + 1, 2 * ((t + 1) % tiles) + 1) for t in range(tiles)]
    along += [(2 * t, 2 * ((t - 1) % tiles)) for t in range(tiles)]
    swap = [(0, 1), (1, 0)]

    edge_own = lax.ppermute(edge_same, both, same)
    edge_other = lax.ppermute(edge_cross, both, cross)
    block_other = lax.ppermute(block, "band", swap)
    slots = lax.all_to_all(
        message.reshape(2 * tiles, 4, LANES), both, split_axis=0, concat_axis=0, tiled=True
    ).reshape(tiles, 8, LANES)

    part = f32(band_levels // 2, cols, rows)
    whole = f32(tracers, band_levels, cols, rows)
    chains = pltpu.VMEM((2, tracers, band_levels, cols, rows), jnp.float32)
    kept, face, to_band, to_cross, to_same = call(
        core_kernel,
        [whole, field, deep, part, part],
        [pltpu.VMEM((levels, cols, rows), jnp.float32)] * 3
        + [chains] * 3
        + [pltpu.VMEM((tracers, cols, rows), jnp.float32), chains],
        10**8,
        32,
        smem=1,
    )(tracer_factor, block, block_other, edge_own, edge_other, slots)
    from_cross = lax.ppermute(to_cross, both, cross)
    from_same = lax.ppermute(to_same, both, along)
    from_band = lax.ppermute(to_band, "band", swap)
    inner, sides = call(finish_kernel, [whole, field], [], 10**7, 16)(
        kept, from_band, block, face
    )
    return call(border_kernel, [whole], [], 10**6, 16)(inner, sides, from_cross, from_same)[0]


def solution(mesh):
    return jax.shard_map(
        functools.partial(per_device, mesh.shape["tile"]),
        mesh=mesh,
        in_specs=(
            P(None, "band", "tile", None),
            P(None, "band", "tile", None),
            P("band", "tile", None),
            P("band", "tile", None),
            P("band", "tile", None),
            P(),
            P("tile"),
            P("tile"),
            P("tile"),
            P("tile", "band"),
        ),
        out_specs=P(None, "band", "tile", None),
        check_vma=False,
    )
```

```python
import functools

import jax
import jax.numpy as jnp
from jax import lax
from jax.experimental import pallas as pl
from jax.experimental.pallas import tpu as pltpu
from jax.sharding import PartitionSpec as P


LANES = 128
PAIR = 32
HALF = 16
MIB = 1 << 20
UNROLL_B = 4
UNROLL_D = 6


def where_am_i():
    return lax.axis_index("band")


def sublane(shape):
    return lax.broadcasted_iota(jnp.int32, shape, len(shape) - 2)


def lane(shape):
    return lax.broadcasted_iota(jnp.int32, shape, len(shape) - 1)


def packed_lines(members, columns):
    place = sublane(members[0].shape)
    lines = [members[0]]
    lines += [pltpu.roll(member, q, 0) for q, member in enumerate(members) if q]
    out = []
    for c in columns:
        one = lines[0]
        for q in range(1, len(members)):
            one = jnp.where(((place - c) & 7) == q, lines[q], one)
        out.append(one)
    return out


def turned(tile, by):
    return pltpu.roll(tile, by % 8, 0) if by % 8 else tile


def first_kernel(out):
    out[...] = jnp.zeros(out.shape, jnp.float32)


def pack_kernel(
    first,
    conc,
    adj,
    east,
    north,
    diff,
    cell,
    value,
    precision,
    weight,
    block,
    edge_same,
    edge_cross,
    message,
    fields,
    done,
):
    tracers, levels, cols, rows = conc.shape
    blocks = cell.shape[0]
    moves = [
        (diff, block.at[1]),
        (east, block.at[2]),
        (north, block.at[3]),
        (adj, block.at[4 : 4 + tracers]),
    ]
    copies = [pltpu.make_async_copy(a, b, done.at[i]) for i, (a, b) in enumerate(moves)]
    for copy in copies:
        copy.start()
    for h in range(3):
        for j in range(blocks):
            fields[h, j, 0:4, :] = weight[4 * h : 4 * h + 4, LANES * j : LANES * (j + 1)]
    for j in range(blocks):
        fields[3, j, 0:1, :] = cell[j : j + 1, :].astype(jnp.float32)
        fields[3, j, 1:2, :] = value[j : j + 1, :]
        fields[3, j, 2:3, :] = precision[j : j + 1, :]
        fields[3, j, 3:4, :] = jnp.zeros((1, LANES), jnp.float32)
    at = lane((4, LANES))
    for h in range(4):
        for j in range(blocks):
            near = pltpu.roll(fields[h, j, 0:4, :], LANES - HALF, 1)
            after = pltpu.roll(fields[h, (j + 1) % blocks, 0:4, :], LANES - HALF, 1)
            fields[h, j, 4:8, :] = jnp.where(at < LANES - HALF, near, after)
    at = lane((8, LANES))
    place = sublane((8, LANES))
    edge = jnp.where(place < 4, float((cols - 1) * rows), float(rows))
    is_cell = ((place & 3) == 0) & (at >= 96)
    for t in range(message.shape[0]):
        j, i = t // 8, t % 8
        parts = []
        for h in range(4):
            if i:
                part = pltpu.roll(fields[h, j], (32 * h - HALF * (i - 1)) % LANES, 1)
            else:
                turn = (32 * h + HALF) % LANES
                before = pltpu.roll(fields[h, (j - 1) % blocks], turn, 1)
                here = pltpu.roll(fields[h, j], turn, 1)
                part = jnp.where((at & 31) < HALF, before, here)
            parts.append(part)
        both = jnp.where(
            at < 64,
            jnp.where(at < 32, parts[0], parts[1]),
            jnp.where(at < 96, parts[2], parts[3]),
        )
        drop = ((at < 112) & (both < edge)) | ((at >= 112) & (both >= edge))
        message[t] = jnp.where(drop & is_cell, -1.0, both)

    band = where_am_i()
    first = jnp.where(band == 0, cols - 1, 0)
    columns = [first, cols - 1 - first]

    def level(j, carry):
        total = conc[0, j]
        for tr in range(1, tracers):
            total = total + conc[tr, j]
        block[0, j] = total
        members = [total, diff[j], east[j]] + [adj[tr, j] for tr in range(tracers)]
        edge_same[j], edge_cross[j] = packed_lines(members, columns)
        return carry

    lax.fori_loop(0, levels, level, 0, unroll=2)
    for copy in copies:
        copy.wait()


def two_parts(x):
    first = x.astype(jnp.bfloat16)
    rest = x - first.astype(jnp.float32)
    second = rest.astype(jnp.bfloat16)
    return first, second


def onehot_dot(x, onehot, dims):
    out = None
    for part in two_parts(x):
        term = lax.dot_general(part, onehot, (dims, ((), ())), preferred_element_type=jnp.float32)
        out = term if out is None else out + term
    return out


def add_soundings(slots, total, forcing):
    levels, cols, rows = total.shape
    band_levels = levels // 2
    sources = slots.shape[0]
    chunk = min(16, sources)
    wide = chunk * PAIR
    block_at = lane((8, LANES)) >> 5

    def gathered(first, h):
        pieces = []
        for v in range(chunk // 4):
            out = None
            for i in range(4):
                part = slots[first + 4 * v + i]
                turn = (32 * (i - h)) % LANES
                part = pltpu.roll(part, turn, 1) if turn else part
                out = part if out is None else jnp.where(block_at == i, part, out)
            pieces.append(out)
        return jnp.concatenate(pieces, axis=1)

    def soundings(c):
        fields = [gathered(c * chunk, h) for h in range(4)]
        cell = fields[3][0:1].astype(jnp.int32)
        value = fields[3][1:2]
        precision = fields[3][2:3]
        y = cell & (rows - 1)
        x = lax.shift_right_arithmetic(cell, rows.bit_length() - 1)
        onehot = jnp.where(sublane((rows, wide)) == y, 1.0, 0.0).astype(jnp.bfloat16)
        on_column = jnp.where(sublane((cols, wide)) == x, 1.0, 0.0)
        weights = []
        for g in range(levels):
            side, l = g // band_levels, g % band_levels
            weights.append(fields[l // 4][4 * side + l % 4 : 4 * side + l % 4 + 1])
        picked = onehot_dot(total[...].reshape(levels * cols, rows), onehot, ((1,), (0,)))
        mean = weights[0] * picked[0:cols]
        for g in range(1, levels):
            mean = mean + weights[g] * picked[g * cols : (g + 1) * cols]
        mean = jnp.sum(mean * on_column, axis=0, keepdims=True)
        misfit = (precision * (mean - value)) * on_column
        spread = jnp.concatenate([weights[g] * misfit for g in range(levels)], axis=0)
        added = onehot_dot(spread, onehot, ((1,), (1,)))
        return added.reshape(levels, cols, rows)

    forcing[...] = soundings(0)
    if sources > chunk:

        def more(c, carry):
            forcing[...] += soundings(c)
            return carry

        lax.fori_loop(1, sources // chunk, more, 0)


def face_parts(e, w, n):
    to_east = jnp.maximum(e, 0.0)
    to_west = jnp.minimum(w, 0.0)
    to_north = jnp.maximum(n, 0.0)
    to_south = jnp.minimum(pltpu.roll(n, 1, 1), 0.0)
    centre = ((1.0 - to_east) + to_west) + (to_south - to_north)
    return centre, to_east, to_west, to_north, to_south


def advected(a, parts):
    centre, to_east, to_west, to_north, to_south = parts
    cols, rows = a.shape
    along = to_east * pltpu.roll(a, cols - 1, 0) - to_west * pltpu.roll(a, 1, 0)
    across = to_north * pltpu.roll(a, rows - 1, 1) - to_south * pltpu.roll(a, 1, 1)
    return centre * a + (along + across)


def chain_level(count, chain, i):
    up = where_am_i() == chain
    return jnp.where(up, i, 2 * count - 1 - i), jnp.where(up, i, count - 1 - i)


def coupling_level(count, chain, i):
    return jnp.where(where_am_i() == chain, i, 2 * count - 2 - i)


class Columns:
    def __init__(self, count, strengths, kinds, inverse, lower, ratio, middle, state):
        self.count, self.strengths, self.kinds = count, strengths, kinds
        self.inverse, self.lower, self.ratio = inverse, lower, ratio
        self.middle, self.state = middle, state
        self.zero = jnp.zeros(state.shape[3:], jnp.float32)

    def both(self, members):
        return [(chain, m) for chain in range(2) for m in range(members)]

    def factorise_and_sweep(self, coupling, source):
        def level(i, carry):
            out = []
            for chain in range(2):
                inward = coupling(chain, i)
                outward, pairs = carry[chain]
                now = []
                for m, amount in enumerate(source(chain, i)):
                    rest, before = pairs[m]
                    k_in = self.strengths[m] * inward[self.kinds[m]]
                    k_out = self.strengths[m] * outward[self.kinds[m]]
                    left = 1.0 + k_out * rest
                    inv = 1.0 / (left + k_in)
                    low = k_out * inv
                    swept = amount * inv + low * before
                    self.inverse[chain, m, i] = inv
                    self.lower[chain, m, i] = low
                    self.ratio[chain, m, i] = k_in * inv
                    self.state[chain, m, i] = swept
                    now.append((left * inv, swept))
                out.append((tuple(inward), tuple(now)))
            return tuple(out)

        zero = self.zero
        outward = tuple(zero for _ in range(max(self.kinds) + 1))
        start = (outward, tuple((zero, zero) for _ in self.strengths))
        ends = lax.fori_loop(0, self.count, level, (start, start), unroll=UNROLL_B)
        for m in range(len(self.strengths)):
            near, far = ends[0][1][m][0], ends[1][1][m][0]
            self.middle[m] = 1.0 / (near + self.ratio[0, m, self.count - 1] * far)

    def sweep(self, members):
        every = self.both(members)

        def level(i, carry):
            out = []
            for chain, m in every:
                before = self.lower[chain, m, i] * carry[len(out)]
                out.append(self.state[chain, m, i] * self.inverse[chain, m, i] + before)
                self.state[chain, m, i] = out[-1]
            return tuple(out)

        lax.fori_loop(0, self.count, level, tuple(self.zero for _ in every), unroll=2)

    def back(self, members):
        last = self.count - 1
        every = self.both(members)
        ends = []
        for chain, m in every:
            mine, others = self.state[chain, m, last], self.state[1 - chain, m, last]
            ends.append((mine + self.ratio[chain, m, last] * others) * self.middle[m])
        for end, (chain, m) in zip(ends, every):
            self.state[chain, m, last] = end

        def level(step, carry):
            i = last - 1 - step
            out = []
            for chain, m in every:
                after = self.ratio[chain, m, i] * carry[len(out)]
                out.append(self.state[chain, m, i] + after)
                self.state[chain, m, i] = out[-1]
            return tuple(out)

        lax.fori_loop(0, last, level, tuple(ends), unroll=2)


def boundary_kernel(
    factor,
    block_own,
    block_other,
    edge_own,
    edge_other,
    slots,
    forcing,
    outer,
    to_cross,
    to_same,
    total,
    diff,
    faces,
    inverse,
    lower,
    ratio,
    middle,
    state,
):
    count, cols, rows = block_own.shape[1:]
    tracers = block_own.shape[0] - 4
    band = where_am_i()
    place = sublane((cols, rows))
    at = lane((cols, rows))
    beyond = jnp.where(band == 0, cols - 1, 0)
    outside = place == beyond
    edge = cols - 1 - beyond
    first = ((place - edge + 1) & 7) < 4
    blocks = (block_own, block_other)
    edges = (edge_own, edge_other)

    def joined(x, y):
        return jnp.where(first, x, pltpu.roll(y, 4, 0))

    def assemble(i, carry):
        for chain in range(2):
            g, l = chain_level(count, chain, i)
            packed = edges[chain][l]
            t, d, e = [
                jnp.where(outside, turned(packed, -q), blocks[chain][q, l]) for q in range(3)
            ]
            total[g] = t
            diff[g] = d
            faces[count * chain + i] = e
        return carry

    lax.fori_loop(0, count, assemble, 0, unroll=2)

    add_soundings(slots, total, forcing)

    def coupling(chain, i):
        d = diff[coupling_level(count, chain, i)]
        return [joined(d, d)]

    def source(chain, i):
        g, l = chain_level(count, chain, i)
        packed = edges[chain][l]
        force = forcing[g]
        amounts = [
            jnp.where(outside, turned(packed, -3 - tr), blocks[chain][4 + tr, l]) + force
            for tr in range(tracers)
        ]
        return [joined(amounts[tr], amounts[tr + 1]) for tr in range(0, tracers, 2)]

    pairs = tracers // 2
    strengths = [jnp.where(first, factor[2 * m], factor[2 * m + 1]) for m in range(pairs)]
    columns = Columns(count, strengths, [0] * pairs, inverse, lower, ratio, middle, state)

    def advect(i, carry):
        for chain in range(2):
            _, l = chain_level(count, chain, i)
            e = faces[count * chain + i]
            n = jnp.where(at == rows - 1, 0.0, blocks[chain][3, l])
            e, n = joined(e, e), joined(n, n)
            parts = face_parts(e, pltpu.roll(e, 1, 0), n)
            for m in range(pairs):
                state[chain, m, i] = advected(state[chain, m, i], parts)
        return carry

    columns.factorise_and_sweep(coupling, source)
    columns.back(pairs)
    lax.fori_loop(0, count, advect, 0, unroll=UNROLL_D)
    columns.sweep(pairs)
    columns.back(pairs)

    def hand_out(j, carry):
        for chain, out in ((1, to_cross), (0, to_same)):
            one = state[chain, 0, 2 * j]
            for q, (m, side) in enumerate(((0, 0), (0, 1), (1, 0), (1, 1))):
                if q:
                    row = pltpu.roll(state[chain, m, 2 * j + side], q, 0)
                    one = jnp.where(((place - edge) & 3) == q, row, one)
            out[j] = one
        return carry

    lax.fori_loop(0, count // 2, hand_out, 0, unroll=2)

    slot = (place - beyond) & 7

    def hand_over(i, carry):
        for chain in range(2):
            g, l = chain_level(count, chain, i)
            force = forcing[g]
            row = jnp.where(band == 0, force[cols - 1 : cols], force[0:1])
            tile = turned(edges[chain][l], -3)
            tile = jnp.where(slot < tracers, tile + row, tile)
            tile = jnp.where(slot == 4, turned(diff[coupling_level(count, chain, i)], 4), tile)
            near = jnp.where(band == 0, turned(force, 4), turned(force, 6))
            outer[count * chain + i] = jnp.where(slot == 5, near, tile)
        return carry

    lax.fori_loop(0, count, hand_over, 0, unroll=2)


def column_kernel(
    factor,
    block_own,
    block_other,
    forcing,
    outer,
    outer_other,
    inner,
    sides,
    inverse,
    lower,
    ratio,
    middle,
    state,
):
    tracers, count, cols, rows = inner.shape
    band = where_am_i()
    place = sublane((cols, rows))
    at = lane((cols, rows))
    beyond = jnp.where(band == 0, cols - 1, 0)
    slot = (place - beyond) & 7
    mine = slot < 4
    blocks = (block_own, block_other)

    def outers(chain, i):
        return outer[count * chain + i], outer_other[count * (1 - chain) + i]

    def coupling(chain, i):
        up = band == chain
        here = blocks[chain][1, jnp.where(up, i, jnp.maximum(count - 2 - i, 0))]
        across = jnp.logical_and(jnp.logical_not(up), i == count - 1)
        d = jnp.where(across, blocks[1 - chain][1, count - 1], here)
        own, got = outers(chain, i)
        d_own = jnp.where(band == 0, own[3:4], own[4:5])
        d_got = jnp.where(band == 0, got[4:5], got[3:4])
        return [d, jnp.where(mine, d_own, d_got)]

    def source(chain, i):
        g, l = chain_level(count, chain, i)
        own, got = outers(chain, i)
        force = jnp.where(
            place == beyond, jnp.where(band == 0, turned(got, 2), turned(got, 4)), forcing[g]
        )
        moved = jnp.where(band == 0, turned(got, 3), turned(got, 5))
        return [blocks[chain][4 + tr, l] + force for tr in range(tracers)] + [
            jnp.where(mine, own, moved)
        ]

    by_row = factor[0]
    for tr in range(1, tracers):
        by_row = jnp.where((slot & 3) == tr, factor[tr], by_row)
    strengths = [factor[tr] for tr in range(tracers)] + [by_row]
    kinds = [0] * tracers + [1]
    columns = Columns(count, strengths, kinds, inverse, lower, ratio, middle, state)

    def parts_of(chain, i):
        _, l = chain_level(count, chain, i)
        own, got = outers(chain, i)
        e = blocks[chain][2, l]
        n = jnp.where(at == rows - 1, 0.0, blocks[chain][3, l])
        before = turned(jnp.where(band == 0, own, got), 2)
        return face_parts(e, jnp.where(place == 0, before, pltpu.roll(e, 1, 0)), n)

    def advect(i, carry):
        for chain in range(2):
            centre, to_east, to_west, to_north, to_south = parts_of(chain, i)
            around = state[chain, tracers, i]
            west = jnp.where(band == 0, around, turned(around, 3))
            east = jnp.where(band == 0, turned(around, 5), around)
            for tr in range(tracers):
                a = state[chain, tr, i]
                a_east = jnp.where(
                    place == cols - 1, turned(east, -1 - tr), pltpu.roll(a, cols - 1, 0)
                )
                a_west = jnp.where(place == 0, turned(west, 1 - tr), pltpu.roll(a, 1, 0))
                along = to_east * a_east - to_west * a_west
                across = to_north * pltpu.roll(a, rows - 1, 1) - to_south * pltpu.roll(a, 1, 1)
                state[chain, tr, i] = centre * a + (along + across)
        return carry

    columns.factorise_and_sweep(coupling, source)
    columns.back(tracers + 1)
    lax.fori_loop(0, count, advect, 0, unroll=2)
    columns.sweep(tracers)
    columns.back(tracers)

    def last(i, carry):
        _, l = chain_level(count, 0, i)
        centre, to_east, to_west, to_north, to_south = parts_of(0, i)
        sides[i] = jnp.where(
            place == cols - 1, to_east, jnp.where(place == 0, -to_west, 0.0)
        )
        to_east = jnp.where(place == cols - 1, 0.0, to_east)
        to_west = jnp.where(place == 0, 0.0, to_west)
        for tr in range(tracers):
            parts = (centre, to_east, to_west, to_north, to_south)
            inner[tr, l] = advected(state[0, tr, i], parts)
        return carry

    lax.fori_loop(0, count, last, 0, unroll=3)


def border_kernel(inner, sides, from_cross, from_same, out):
    tracers, count, cols, rows = inner.shape
    band = where_am_i()
    place = sublane((cols, rows))

    def pair(j, carry):
        cross, same = from_cross[j], from_same[j]
        westward = jnp.where(band == 0, cross, same)
        eastward = jnp.where(band == 0, same, cross)
        for side in range(2):
            i = 2 * j + side
            l = jnp.where(band == 0, i, count - 1 - i)
            for tr in range(tracers):
                q = 4 * (tr & 1) + 2 * (tr >> 1) + side
                beyond = jnp.where(place == 0, turned(westward, 1 - q), turned(eastward, -1 - q))
                out[tr, l] = inner[tr, l] + sides[i] * beyond
        return carry

    lax.fori_loop(0, count // 2, pair, 0, unroll=2)


def f32(*shape):
    return jax.ShapeDtypeStruct(shape, jnp.float32)


def call(kernel, outs, scratch, ops, limit, smem=0, moved=None):
    vmem = pl.BlockSpec(memory_space=pltpu.VMEM)
    scalars = pl.BlockSpec(memory_space=pltpu.SMEM)

    def run(*args):
        size = moved or sum(4 * a.size for a in args) + sum(4 * o.size for o in outs)
        return pl.pallas_call(
            kernel,
            out_shape=outs,
            in_specs=[scalars] * smem + [vmem] * (len(args) - smem),
            out_specs=[vmem] * len(outs),
            scratch_shapes=scratch,
            compiler_params=pltpu.CompilerParams(vmem_limit_bytes=limit * MIB),
            cost_estimate=pl.CostEstimate(flops=ops, bytes_accessed=size, transcendentals=0),
        )(*args)

    return run


def per_device(
    tiles,
    concentration,
    adjoint_later,
    courant_east,
    courant_north,
    diffusivity,
    tracer_factor,
    sounding_cell,
    sounding_value,
    sounding_precision,
    sounding_weight,
):
    tracers, band_levels, cols, rows = concentration.shape
    levels = 2 * band_levels
    blocks = sounding_cell.shape[0] // LANES
    field = f32(band_levels, cols, rows)
    deep = f32(levels, cols, rows)

    first = call(first_kernel, [f32(8, LANES)], [], 10**9, 8)()[0]
    block, edge_same, edge_cross, message = call(
        pack_kernel,
        [f32(4 + tracers, band_levels, cols, rows), field, field, f32(tiles, 8, LANES)],
        [pltpu.VMEM((4, blocks, 8, LANES), jnp.float32), pltpu.SemaphoreType.DMA((4,))],
        10**6,
        16,
    )(
        first,
        concentration,
        adjoint_later,
        courant_east,
        courant_north,
        diffusivity,
        sounding_cell.reshape(blocks, LANES),
        sounding_value.reshape(blocks, LANES),
        sounding_precision.reshape(blocks, LANES),
        sounding_weight.T,
    )

    both = ("tile", "band")
    same = [(2 * t, 2 * ((t + 1) % tiles)) for t in range(tiles)]
    same += [(2 * t + 1, 2 * ((t - 1) % tiles) + 1) for t in range(tiles)]
    cross = [(2 * t + 1, 2 * ((t + 1) % tiles)) for t in range(tiles)]
    cross += [(2 * t, 2 * ((t - 1) % tiles) + 1) for t in range(tiles)]
    along = [(2 * t + 1, 2 * ((t + 1) % tiles) + 1) for t in range(tiles)]
    along += [(2 * t, 2 * ((t - 1) % tiles)) for t in range(tiles)]
    swap = [(0, 1), (1, 0)]

    edge_own = lax.ppermute(edge_same, both, same)
    edge_other = lax.ppermute(edge_cross, both, cross)
    block_other = lax.ppermute(block, "band", swap)
    slots = lax.all_to_all(
        message.reshape(2 * tiles, 4, LANES), both, split_axis=0, concat_axis=0, tiled=True
    ).reshape(tiles, 8, LANES)

    part = f32(band_levels // 2, cols, rows)
    whole = f32(tracers, band_levels, cols, rows)

    def room(members):
        chains = pltpu.VMEM((2, members, band_levels, cols, rows), jnp.float32)
        return [chains] * 3 + [pltpu.VMEM((members, cols, rows), jnp.float32), chains]

    forcing, outer, to_cross, to_same = call(
        boundary_kernel,
        [deep, deep, part, part],
        [pltpu.VMEM((levels, cols, rows), jnp.float32)] * 3 + room(tracers // 2),
        10**8,
        24,
        smem=1,
    )(tracer_factor, block, block_other, edge_own, edge_other, slots)
    from_cross = lax.ppermute(to_cross, both, cross)
    from_same = lax.ppermute(to_same, both, along)
    outer_other = lax.ppermute(outer, "band", swap)
    inner, sides = call(
        column_kernel, [whole, field], room(tracers + 1), 10**9, 24, smem=1
    )(tracer_factor, block, block_other, forcing, outer, outer_other)
    return call(border_kernel, [whole], [], 10**6, 16)(inner, sides, from_cross, from_same)[0]


def solution(mesh):
    return jax.shard_map(
        functools.partial(per_device, mesh.shape["tile"]),
        mesh=mesh,
        in_specs=(
            P(None, "band", "tile", None),
            P(None, "band", "tile", None),
            P("band", "tile", None),
            P("band", "tile", None),
            P("band", "tile", None),
            P(),
            P("tile"),
            P("tile"),
            P("tile"),
            P("tile", "band"),
        ),
        out_specs=P(None, "band", "tile", None),
        check_vma=False,
    )
```

```python
import functools

import jax
import jax.numpy as jnp
from jax import lax
from jax.experimental import pallas as pl
from jax.experimental.pallas import tpu as pltpu
from jax.sharding import PartitionSpec as P


LANES = 128
PAIR = 32
HALF = 16
MIB = 1 << 20
UNROLL_B = 4
UNROLL_D = 12


def where_am_i():
    return lax.axis_index("band")


def sublane(shape):
    return lax.broadcasted_iota(jnp.int32, shape, len(shape) - 2)


def lane(shape):
    return lax.broadcasted_iota(jnp.int32, shape, len(shape) - 1)


def packed_lines(members, columns):
    place = sublane(members[0].shape)
    lines = [members[0]]
    lines += [pltpu.roll(member, q, 0) for q, member in enumerate(members) if q]
    out = []
    for c in columns:
        one = lines[0]
        for q in range(1, len(members)):
            one = jnp.where(((place - c) & 7) == q, lines[q], one)
        out.append(one)
    return out


def turned(tile, by):
    return pltpu.roll(tile, by % 8, 0) if by % 8 else tile


def first_kernel(out):
    out[...] = jnp.zeros(out.shape, jnp.float32)


def pack_kernel(
    first,
    conc,
    adj,
    east,
    north,
    diff,
    cell,
    value,
    precision,
    weight,
    block,
    edge_same,
    edge_cross,
    message,
    fields,
):
    tracers, levels, cols, rows = conc.shape
    blocks = cell.shape[0]
    for h in range(3):
        for j in range(blocks):
            fields[h, j, 0:4, :] = weight[4 * h : 4 * h + 4, LANES * j : LANES * (j + 1)]
    for j in range(blocks):
        fields[3, j, 0:1, :] = cell[j : j + 1, :].astype(jnp.float32)
        fields[3, j, 1:2, :] = value[j : j + 1, :]
        fields[3, j, 2:3, :] = precision[j : j + 1, :]
        fields[3, j, 3:4, :] = jnp.zeros((1, LANES), jnp.float32)
    at = lane((4, LANES))
    for h in range(4):
        for j in range(blocks):
            near = pltpu.roll(fields[h, j, 0:4, :], LANES - HALF, 1)
            after = pltpu.roll(fields[h, (j + 1) % blocks, 0:4, :], LANES - HALF, 1)
            fields[h, j, 4:8, :] = jnp.where(at < LANES - HALF, near, after)
    at = lane((8, LANES))
    place = sublane((8, LANES))
    edge = jnp.where(place < 4, float((cols - 1) * rows), float(rows))
    is_cell = ((place & 3) == 0) & (at >= 96)
    for t in range(message.shape[0]):
        j, i = t // 8, t % 8
        parts = []
        for h in range(4):
            if i:
                part = pltpu.roll(fields[h, j], (32 * h - HALF * (i - 1)) % LANES, 1)
            else:
                turn = (32 * h + HALF) % LANES
                before = pltpu.roll(fields[h, (j - 1) % blocks], turn, 1)
                here = pltpu.roll(fields[h, j], turn, 1)
                part = jnp.where((at & 31) < HALF, before, here)
            parts.append(part)
        both = jnp.where(
            at < 64,
            jnp.where(at < 32, parts[0], parts[1]),
            jnp.where(at < 96, parts[2], parts[3]),
        )
        drop = ((at < 112) & (both < edge)) | ((at >= 112) & (both >= edge))
        message[t] = jnp.where(drop & is_cell, -1.0, both)

    band = where_am_i()
    first = jnp.where(band == 0, cols - 1, 0)
    columns = [first, cols - 1 - first]

    def level(j, carry):
        total = conc[0, j]
        for tr in range(1, tracers):
            total = total + conc[tr, j]
        block[0, j] = total
        for q, field in enumerate((diff, east, north)):
            block[1 + q, j] = field[j]
        for tr in range(tracers):
            block[4 + tr, j] = adj[tr, j]
        members = [total, diff[j], east[j]] + [adj[tr, j] for tr in range(tracers)]
        edge_same[j], edge_cross[j] = packed_lines(members, columns)
        return carry

    lax.fori_loop(0, levels, level, 0, unroll=12)


def two_parts(x):
    first = x.astype(jnp.bfloat16)
    rest = x - first.astype(jnp.float32)
    second = rest.astype(jnp.bfloat16)
    return first, second


def onehot_dot(x, onehot, dims):
    out = None
    for part in two_parts(x):
        term = lax.dot_general(part, onehot, (dims, ((), ())), preferred_element_type=jnp.float32)
        out = term if out is None else out + term
    return out


def add_soundings(slots, total, forcing):
    levels, cols, rows = total.shape
    band_levels = levels // 2
    sources = slots.shape[0]
    chunk = min(16, sources)
    wide = chunk * PAIR
    block_at = lane((8, LANES)) >> 5

    def gathered(first, h):
        pieces = []
        for v in range(chunk // 4):
            out = None
            for i in range(4):
                part = slots[first + 4 * v + i]
                turn = (32 * (i - h)) % LANES
                part = pltpu.roll(part, turn, 1) if turn else part
                out = part if out is None else jnp.where(block_at == i, part, out)
            pieces.append(out)
        return jnp.concatenate(pieces, axis=1)

    def soundings(c):
        fields = [gathered(c * chunk, h) for h in range(4)]
        cell = fields[3][0:1].astype(jnp.int32)
        value = fields[3][1:2]
        precision = fields[3][2:3]
        y = cell & (rows - 1)
        x = lax.shift_right_arithmetic(cell, rows.bit_length() - 1)
        onehot = jnp.where(sublane((rows, wide)) == y, 1.0, 0.0).astype(jnp.bfloat16)
        on_column = jnp.where(sublane((cols, wide)) == x, 1.0, 0.0)
        weights = []
        for g in range(levels):
            side, l = g // band_levels, g % band_levels
            weights.append(fields[l // 4][4 * side + l % 4 : 4 * side + l % 4 + 1])
        picked = onehot_dot(total[...].reshape(levels * cols, rows), onehot, ((1,), (0,)))
        mean = weights[0] * picked[0:cols]
        for g in range(1, levels):
            mean = mean + weights[g] * picked[g * cols : (g + 1) * cols]
        mean = jnp.sum(mean * on_column, axis=0, keepdims=True)
        misfit = (precision * (mean - value)) * on_column
        spread = jnp.concatenate([weights[g] * misfit for g in range(levels)], axis=0)
        added = onehot_dot(spread, onehot, ((1,), (1,)))
        return added.reshape(levels, cols, rows)

    forcing[...] = soundings(0)
    if sources > chunk:

        def more(c, carry):
            forcing[...] += soundings(c)
            return carry

        lax.fori_loop(1, sources // chunk, more, 0)


def face_parts(e, w, n):
    to_east = jnp.maximum(e, 0.0)
    to_west = jnp.minimum(w, 0.0)
    to_north = jnp.maximum(n, 0.0)
    to_south = jnp.minimum(pltpu.roll(n, 1, 1), 0.0)
    centre = ((1.0 - to_east) + to_west) + (to_south - to_north)
    return centre, to_east, to_west, to_north, to_south


def advected(a, parts):
    centre, to_east, to_west, to_north, to_south = parts
    cols, rows = a.shape
    along = to_east * pltpu.roll(a, cols - 1, 0) - to_west * pltpu.roll(a, 1, 0)
    across = to_north * pltpu.roll(a, rows - 1, 1) - to_south * pltpu.roll(a, 1, 1)
    return centre * a + (along + across)


def chain_level(count, chain, i):
    up = where_am_i() == chain
    return jnp.where(up, i, 2 * count - 1 - i), jnp.where(up, i, count - 1 - i)


def coupling_level(count, chain, i):
    return jnp.where(where_am_i() == chain, i, 2 * count - 2 - i)


class Columns:
    def __init__(self, count, strengths, kinds, inverse, lower, ratio, middle, state):
        self.count, self.strengths, self.kinds = count, strengths, kinds
        self.inverse, self.lower, self.ratio = inverse, lower, ratio
        self.middle, self.state = middle, state
        self.zero = jnp.zeros(state.shape[3:], jnp.float32)

    def both(self, members):
        return [(chain, m) for chain in range(2) for m in range(members)]

    def factorise_and_sweep(self, coupling, source):
        def level(i, carry):
            out = []
            for chain in range(2):
                inward = coupling(chain, i)
                outward, pairs = carry[chain]
                now = []
                for m, amount in enumerate(source(chain, i)):
                    rest, before = pairs[m]
                    k_in = self.strengths[m] * inward[self.kinds[m]]
                    k_out = self.strengths[m] * outward[self.kinds[m]]
                    left = 1.0 + k_out * rest
                    inv = 1.0 / (left + k_in)
                    low = k_out * inv
                    swept = amount * inv + low * before
                    self.inverse[chain, m, i] = inv
                    self.lower[chain, m, i] = low
                    self.ratio[chain, m, i] = k_in * inv
                    self.state[chain, m, i] = swept
                    now.append((left * inv, swept))
                out.append((tuple(inward), tuple(now)))
            return tuple(out)

        zero = self.zero
        outward = tuple(zero for _ in range(max(self.kinds) + 1))
        start = (outward, tuple((zero, zero) for _ in self.strengths))
        ends = lax.fori_loop(0, self.count, level, (start, start), unroll=UNROLL_B)
        for m in range(len(self.strengths)):
            near, far = ends[0][1][m][0], ends[1][1][m][0]
            self.middle[m] = 1.0 / (near + self.ratio[0, m, self.count - 1] * far)

    def sweep(self, members):
        every = self.both(members)

        def level(i, carry):
            out = []
            for chain, m in every:
                before = self.lower[chain, m, i] * carry[len(out)]
                out.append(self.state[chain, m, i] * self.inverse[chain, m, i] + before)
                self.state[chain, m, i] = out[-1]
            return tuple(out)

        lax.fori_loop(0, self.count, level, tuple(self.zero for _ in every), unroll=4)

    def back(self, members):
        last = self.count - 1
        every = self.both(members)
        ends = []
        for chain, m in every:
            mine, others = self.state[chain, m, last], self.state[1 - chain, m, last]
            ends.append((mine + self.ratio[chain, m, last] * others) * self.middle[m])
        for end, (chain, m) in zip(ends, every):
            self.state[chain, m, last] = end

        def level(step, carry):
            i = last - 1 - step
            out = []
            for chain, m in every:
                after = self.ratio[chain, m, i] * carry[len(out)]
                out.append(self.state[chain, m, i] + after)
                self.state[chain, m, i] = out[-1]
            return tuple(out)

        lax.fori_loop(0, last, level, tuple(ends), unroll=4)


def boundary_kernel(
    factor,
    block_own,
    block_other,
    edge_own,
    edge_other,
    slots,
    forcing,
    outer,
    to_cross,
    to_same,
    total,
    diff,
    faces,
    inverse,
    lower,
    ratio,
    middle,
    state,
):
    count, cols, rows = block_own.shape[1:]
    tracers = block_own.shape[0] - 4
    band = where_am_i()
    place = sublane((cols, rows))
    at = lane((cols, rows))
    beyond = jnp.where(band == 0, cols - 1, 0)
    outside = place == beyond
    edge = cols - 1 - beyond
    first = ((place - edge + 1) & 7) < 4
    blocks = (block_own, block_other)
    edges = (edge_own, edge_other)

    def joined(x, y):
        return jnp.where(first, x, pltpu.roll(y, 4, 0))

    def assemble(i, carry):
        for chain in range(2):
            g, l = chain_level(count, chain, i)
            packed = edges[chain][l]
            t, d, e = [
                jnp.where(outside, turned(packed, -q), blocks[chain][q, l]) for q in range(3)
            ]
            total[g] = t
            diff[g] = d
            faces[count * chain + i] = e
        return carry

    lax.fori_loop(0, count, assemble, 0, unroll=2)

    add_soundings(slots, total, forcing)

    def coupling(chain, i):
        d = diff[coupling_level(count, chain, i)]
        return [joined(d, d)]

    def source(chain, i):
        g, l = chain_level(count, chain, i)
        packed = edges[chain][l]
        force = forcing[g]
        amounts = [
            jnp.where(outside, turned(packed, -3 - tr), blocks[chain][4 + tr, l]) + force
            for tr in range(tracers)
        ]
        return [joined(amounts[tr], amounts[tr + 1]) for tr in range(0, tracers, 2)]

    pairs = tracers // 2
    strengths = [jnp.where(first, factor[2 * m], factor[2 * m + 1]) for m in range(pairs)]
    columns = Columns(count, strengths, [0] * pairs, inverse, lower, ratio, middle, state)

    def advect(i, carry):
        for chain in range(2):
            _, l = chain_level(count, chain, i)
            e = faces[count * chain + i]
            n = jnp.where(at == rows - 1, 0.0, blocks[chain][3, l])
            e, n = joined(e, e), joined(n, n)
            parts = face_parts(e, pltpu.roll(e, 1, 0), n)
            for m in range(pairs):
                state[chain, m, i] = advected(state[chain, m, i], parts)
        return carry

    columns.factorise_and_sweep(coupling, source)
    columns.back(pairs)
    lax.fori_loop(0, count, advect, 0, unroll=UNROLL_D)
    columns.sweep(pairs)
    columns.back(pairs)

    def hand_out(j, carry):
        for chain, out in ((1, to_cross), (0, to_same)):
            one = state[chain, 0, 2 * j]
            for q, (m, side) in enumerate(((0, 0), (0, 1), (1, 0), (1, 1))):
                if q:
                    row = pltpu.roll(state[chain, m, 2 * j + side], q, 0)
                    one = jnp.where(((place - edge) & 3) == q, row, one)
            out[j] = one
        return carry

    lax.fori_loop(0, count // 2, hand_out, 0, unroll=6)

    slot = (place - beyond) & 7

    def hand_over(i, carry):
        for chain in range(2):
            g, l = chain_level(count, chain, i)
            force = forcing[g]
            row = jnp.where(band == 0, force[cols - 1 : cols], force[0:1])
            tile = turned(edges[chain][l], -3)
            tile = jnp.where(slot < tracers, tile + row, tile)
            tile = jnp.where(slot == 4, turned(diff[coupling_level(count, chain, i)], 4), tile)
            near = jnp.where(band == 0, turned(force, 4), turned(force, 6))
            outer[count * chain + i] = jnp.where(slot == 5, near, tile)
        return carry

    lax.fori_loop(0, count, hand_over, 0, unroll=6)


def column_kernel(
    factor,
    block_own,
    block_other,
    forcing,
    outer,
    outer_other,
    inner,
    sides,
    inverse,
    lower,
    ratio,
    middle,
    state,
):
    tracers, count, cols, rows = inner.shape
    band = where_am_i()
    place = sublane((cols, rows))
    at = lane((cols, rows))
    beyond = jnp.where(band == 0, cols - 1, 0)
    slot = (place - beyond) & 7
    mine = slot < 4
    blocks = (block_own, block_other)

    def outers(chain, i):
        return outer[count * chain + i], outer_other[count * (1 - chain) + i]

    def coupling(chain, i):
        up = band == chain
        here = blocks[chain][1, jnp.where(up, i, jnp.maximum(count - 2 - i, 0))]
        across = jnp.logical_and(jnp.logical_not(up), i == count - 1)
        d = jnp.where(across, blocks[1 - chain][1, count - 1], here)
        own, got = outers(chain, i)
        d_own = jnp.where(band == 0, own[3:4], own[4:5])
        d_got = jnp.where(band == 0, got[4:5], got[3:4])
        return [d, jnp.where(mine, d_own, d_got)]

    def source(chain, i):
        g, l = chain_level(count, chain, i)
        own, got = outers(chain, i)
        force = jnp.where(
            place == beyond, jnp.where(band == 0, turned(got, 2), turned(got, 4)), forcing[g]
        )
        moved = jnp.where(band == 0, turned(got, 3), turned(got, 5))
        return [blocks[chain][4 + tr, l] + force for tr in range(tracers)] + [
            jnp.where(mine, own, moved)
        ]

    by_row = factor[0]
    for tr in range(1, tracers):
        by_row = jnp.where((slot & 3) == tr, factor[tr], by_row)
    strengths = [factor[tr] for tr in range(tracers)] + [by_row]
    kinds = [0] * tracers + [1]
    columns = Columns(count, strengths, kinds, inverse, lower, ratio, middle, state)

    def parts_of(chain, i):
        _, l = chain_level(count, chain, i)
        own, got = outers(chain, i)
        e = blocks[chain][2, l]
        n = jnp.where(at == rows - 1, 0.0, blocks[chain][3, l])
        before = turned(jnp.where(band == 0, own, got), 2)
        return face_parts(e, jnp.where(place == 0, before, pltpu.roll(e, 1, 0)), n)

    def advect(i, carry):
        for chain in range(2):
            centre, to_east, to_west, to_north, to_south = parts_of(chain, i)
            around = state[chain, tracers, i]
            west = jnp.where(band == 0, around, turned(around, 3))
            east = jnp.where(band == 0, turned(around, 5), around)
            for tr in range(tracers):
                a = state[chain, tr, i]
                a_east = jnp.where(
                    place == cols - 1, turned(east, -1 - tr), pltpu.roll(a, cols - 1, 0)
                )
                a_west = jnp.where(place == 0, turned(west, 1 - tr), pltpu.roll(a, 1, 0))
                along = to_east * a_east - to_west * a_west
                across = to_north * pltpu.roll(a, rows - 1, 1) - to_south * pltpu.roll(a, 1, 1)
                state[chain, tr, i] = centre * a + (along + across)
        return carry

    columns.factorise_and_sweep(coupling, source)
    columns.back(tracers + 1)
    lax.fori_loop(0, count, advect, 0, unroll=4)
    columns.sweep(tracers)
    columns.back(tracers)

    def last(i, carry):
        _, l = chain_level(count, 0, i)
        centre, to_east, to_west, to_north, to_south = parts_of(0, i)
        sides[i] = jnp.where(
            place == cols - 1, to_east, jnp.where(place == 0, -to_west, 0.0)
        )
        to_east = jnp.where(place == cols - 1, 0.0, to_east)
        to_west = jnp.where(place == 0, 0.0, to_west)
        for tr in range(tracers):
            parts = (centre, to_east, to_west, to_north, to_south)
            inner[tr, l] = advected(state[0, tr, i], parts)
        return carry

    lax.fori_loop(0, count, last, 0, unroll=3)


def border_kernel(inner, sides, from_cross, from_same, out, ready, done):
    tracers, count, cols, rows = inner.shape
    band = where_am_i()
    place = sublane((cols, rows))
    copies = []
    for j in range(count // 2):
        cross, same = from_cross[j], from_same[j]
        westward = jnp.where(band == 0, cross, same)
        eastward = jnp.where(band == 0, same, cross)
        for side in range(2):
            i = 2 * j + side
            l = jnp.where(band == 0, i, count - 1 - i)
            for tr in range(tracers):
                q = 4 * (tr & 1) + 2 * (tr >> 1) + side
                beyond = jnp.where(place == 0, turned(westward, 1 - q), turned(eastward, -1 - q))
                ready[tr, l] = inner[tr, l] + sides[i] * beyond
        low = jnp.where(band == 0, 2 * j, count - 2 - 2 * j)
        part = (slice(None), pl.ds(low, 2))
        copies.append(pltpu.make_async_copy(ready.at[part], out.at[part], done.at[j]))
        copies[-1].start()
    for copy in copies:
        copy.wait()


def f32(*shape):
    return jax.ShapeDtypeStruct(shape, jnp.float32)


def call(kernel, outs, scratch, ops, limit, smem=0, moved=None, out_space=pltpu.VMEM):
    vmem = pl.BlockSpec(memory_space=pltpu.VMEM)
    scalars = pl.BlockSpec(memory_space=pltpu.SMEM)

    def run(*args):
        size = moved or sum(4 * a.size for a in args) + sum(4 * o.size for o in outs)
        return pl.pallas_call(
            kernel,
            out_shape=outs,
            in_specs=[scalars] * smem + [vmem] * (len(args) - smem),
            out_specs=[pl.BlockSpec(memory_space=out_space)] * len(outs),
            scratch_shapes=scratch,
            compiler_params=pltpu.CompilerParams(vmem_limit_bytes=limit * MIB),
            cost_estimate=pl.CostEstimate(flops=ops, bytes_accessed=size, transcendentals=0),
        )(*args)

    return run


def per_device(
    tiles,
    concentration,
    adjoint_later,
    courant_east,
    courant_north,
    diffusivity,
    tracer_factor,
    sounding_cell,
    sounding_value,
    sounding_precision,
    sounding_weight,
):
    tracers, band_levels, cols, rows = concentration.shape
    levels = 2 * band_levels
    blocks = sounding_cell.shape[0] // LANES
    field = f32(band_levels, cols, rows)
    deep = f32(levels, cols, rows)

    first = call(first_kernel, [f32(8, LANES)], [], 10**9, 8)()[0]
    block, edge_same, edge_cross, message = call(
        pack_kernel,
        [f32(4 + tracers, band_levels, cols, rows), field, field, f32(tiles, 8, LANES)],
        [pltpu.VMEM((4, blocks, 8, LANES), jnp.float32)],
        10**6,
        16,
    )(
        first,
        concentration,
        adjoint_later,
        courant_east,
        courant_north,
        diffusivity,
        sounding_cell.reshape(blocks, LANES),
        sounding_value.reshape(blocks, LANES),
        sounding_precision.reshape(blocks, LANES),
        sounding_weight.T,
    )

    both = ("tile", "band")
    same = [(2 * t, 2 * ((t + 1) % tiles)) for t in range(tiles)]
    same += [(2 * t + 1, 2 * ((t - 1) % tiles) + 1) for t in range(tiles)]
    cross = [(2 * t + 1, 2 * ((t + 1) % tiles)) for t in range(tiles)]
    cross += [(2 * t, 2 * ((t - 1) % tiles) + 1) for t in range(tiles)]
    along = [(2 * t + 1, 2 * ((t + 1) % tiles) + 1) for t in range(tiles)]
    along += [(2 * t, 2 * ((t - 1) % tiles)) for t in range(tiles)]
    swap = [(0, 1), (1, 0)]

    edge_own = lax.ppermute(edge_same, both, same)
    edge_other = lax.ppermute(edge_cross, both, cross)
    block_other = lax.ppermute(block, "band", swap)
    slots = lax.all_to_all(
        message.reshape(2 * tiles, 4, LANES), both, split_axis=0, concat_axis=0, tiled=True
    ).reshape(tiles, 8, LANES)

    part = f32(band_levels // 2, cols, rows)
    whole = f32(tracers, band_levels, cols, rows)

    def room(members):
        chains = pltpu.VMEM((2, members, band_levels, cols, rows), jnp.float32)
        return [chains] * 3 + [pltpu.VMEM((members, cols, rows), jnp.float32), chains]

    forcing, outer, to_cross, to_same = call(
        boundary_kernel,
        [deep, deep, part, part],
        [pltpu.VMEM((levels, cols, rows), jnp.float32)] * 3 + room(tracers // 2),
        10**8,
        24,
        smem=1,
    )(tracer_factor, block, block_other, edge_own, edge_other, slots)
    from_cross = lax.ppermute(to_cross, both, cross)
    from_same = lax.ppermute(to_same, both, along)
    outer_other = lax.ppermute(outer, "band", swap)
    inner, sides = call(
        column_kernel, [whole, field], room(tracers + 1), 10**9, 24, smem=1
    )(tracer_factor, block, block_other, forcing, outer, outer_other)
    ready = pltpu.VMEM((tracers, band_levels, cols, rows), jnp.float32)
    done = pltpu.SemaphoreType.DMA((band_levels // 2,))
    return call(border_kernel, [whole], [ready, done], 10**6, 16, out_space=pl.ANY)(
        inner, sides, from_cross, from_same
    )[0]


def solution(mesh):
    return jax.shard_map(
        functools.partial(per_device, mesh.shape["tile"]),
        mesh=mesh,
        in_specs=(
            P(None, "band", "tile", None),
            P(None, "band", "tile", None),
            P("band", "tile", None),
            P("band", "tile", None),
            P("band", "tile", None),
            P(),
            P("tile"),
            P("tile"),
            P("tile"),
            P("tile", "band"),
        ),
        out_specs=P(None, "band", "tile", None),
        check_vma=False,
    )
```

```python
import functools

import jax
import jax.numpy as jnp
from jax import lax
from jax.experimental import pallas as pl
from jax.experimental.pallas import tpu as pltpu
from jax.sharding import PartitionSpec as P


LANES = 128
PAIR = 32
HALF = 16
MIB = 1 << 20


def where_am_i():
    return lax.axis_index("band")


def sublane(shape):
    return lax.broadcasted_iota(jnp.int32, shape, len(shape) - 2)


def lane(shape):
    return lax.broadcasted_iota(jnp.int32, shape, len(shape) - 1)


def packed_lines(members, columns):
    place = sublane(members[0].shape)
    lines = [members[0]]
    lines += [pltpu.roll(member, q, 0) for q, member in enumerate(members) if q]
    out = []
    for c in columns:
        one = lines[0]
        for q in range(1, len(members)):
            one = jnp.where(((place - c) & 7) == q, lines[q], one)
        out.append(one)
    return out


def turned(tile, by):
    return pltpu.roll(tile, by % 8, 0) if by % 8 else tile


def first_kernel(out):
    out[...] = jnp.zeros(out.shape, jnp.float32)


def pack_kernel(
    first,
    conc,
    adj,
    east,
    north,
    diff,
    cell,
    value,
    precision,
    weight,
    block,
    edge_same,
    edge_cross,
    message,
    fields,
):
    tracers, levels, cols, rows = conc.shape
    blocks = cell.shape[0]
    for h in range(3):
        for j in range(blocks):
            fields[h, j, 0:4, :] = weight[4 * h : 4 * h + 4, LANES * j : LANES * (j + 1)]
    for j in range(blocks):
        fields[3, j, 0:1, :] = cell[j : j + 1, :].astype(jnp.float32)
        fields[3, j, 1:2, :] = value[j : j + 1, :]
        fields[3, j, 2:3, :] = precision[j : j + 1, :]
        fields[3, j, 3:4, :] = jnp.zeros((1, LANES), jnp.float32)
    at = lane((4, LANES))
    for h in range(4):
        for j in range(blocks):
            near = pltpu.roll(fields[h, j, 0:4, :], LANES - HALF, 1)
            after = pltpu.roll(fields[h, (j + 1) % blocks, 0:4, :], LANES - HALF, 1)
            fields[h, j, 4:8, :] = jnp.where(at < LANES - HALF, near, after)
    at = lane((8, LANES))
    place = sublane((8, LANES))
    edge = jnp.where(place < 4, float((cols - 1) * rows), float(rows))
    is_cell = ((place & 3) == 0) & (at >= 96)
    for t in range(message.shape[0]):
        j, i = t // 8, t % 8
        parts = []
        for h in range(4):
            if i:
                part = pltpu.roll(fields[h, j], (32 * h - HALF * (i - 1)) % LANES, 1)
            else:
                turn = (32 * h + HALF) % LANES
                before = pltpu.roll(fields[h, (j - 1) % blocks], turn, 1)
                here = pltpu.roll(fields[h, j], turn, 1)
                part = jnp.where((at & 31) < HALF, before, here)
            parts.append(part)
        both = jnp.where(
            at < 64,
            jnp.where(at < 32, parts[0], parts[1]),
            jnp.where(at < 96, parts[2], parts[3]),
        )
        drop = ((at < 112) & (both < edge)) | ((at >= 112) & (both >= edge))
        message[t] = jnp.where(drop & is_cell, -1.0, both)

    band = where_am_i()
    first = jnp.where(band == 0, cols - 1, 0)
    columns = [first, cols - 1 - first]

    def level(j, carry):
        total = conc[0, j]
        for tr in range(1, tracers):
            total = total + conc[tr, j]
        block[0, j] = total
        for q, field in enumerate((diff, east, north)):
            block[1 + q, j] = field[j]
        for tr in range(tracers):
            block[4 + tr, j] = adj[tr, j]
        members = [total, diff[j], east[j]] + [adj[tr, j] for tr in range(tracers)]
        edge_same[j], edge_cross[j] = packed_lines(members, columns)
        return carry

    lax.fori_loop(0, levels, level, 0, unroll=levels)


def two_parts(x):
    first = x.astype(jnp.bfloat16)
    rest = x - first.astype(jnp.float32)
    second = rest.astype(jnp.bfloat16)
    return first, second


def onehot_dot(x, onehot, dims):
    many = x.shape[0]
    parts = jnp.concatenate(two_parts(x), axis=0)
    out = lax.dot_general(parts, onehot, (dims, ((), ())), preferred_element_type=jnp.float32)
    return out[:many] + out[many:]


def add_soundings(slots, total, forcing):
    levels, cols, rows = total.shape
    band_levels = levels // 2
    sources = slots.shape[0]
    chunk = min(16, sources)
    wide = chunk * PAIR
    block_at = lane((8, LANES)) >> 5

    def gathered(first, h):
        pieces = []
        for v in range(chunk // 4):
            out = None
            for i in range(4):
                part = slots[first + 4 * v + i]
                turn = (32 * (i - h)) % LANES
                part = pltpu.roll(part, turn, 1) if turn else part
                out = part if out is None else jnp.where(block_at == i, part, out)
            pieces.append(out)
        return jnp.concatenate(pieces, axis=1)

    def soundings(c):
        fields = [gathered(c * chunk, h) for h in range(4)]
        cell = fields[3][0:1].astype(jnp.int32)
        value = fields[3][1:2]
        precision = fields[3][2:3]
        y = cell & (rows - 1)
        x = lax.shift_right_arithmetic(cell, rows.bit_length() - 1)
        onehot = jnp.where(sublane((rows, wide)) == y, 1.0, 0.0).astype(jnp.bfloat16)
        on_column = jnp.where(sublane((cols, wide)) == x, 1.0, 0.0)
        weights = []
        for g in range(levels):
            side, l = g // band_levels, g % band_levels
            weights.append(fields[l // 4][4 * side + l % 4 : 4 * side + l % 4 + 1])
        picked = onehot_dot(total[...].reshape(levels * cols, rows), onehot, ((1,), (0,)))
        mean = weights[0] * picked[0:cols]
        for g in range(1, levels):
            mean = mean + weights[g] * picked[g * cols : (g + 1) * cols]
        mean = jnp.sum(mean * on_column, axis=0, keepdims=True)
        misfit = (precision * (mean - value)) * on_column
        spread = jnp.concatenate([weights[g] * misfit for g in range(levels)], axis=0)
        added = onehot_dot(spread, onehot, ((1,), (1,)))
        return added.reshape(levels, cols, rows)

    forcing[...] = soundings(0)
    if sources > chunk:

        def more(c, carry):
            forcing[...] += soundings(c)
            return carry

        lax.fori_loop(1, sources // chunk, more, 0)


def face_parts(e, w, n):
    to_east = jnp.maximum(e, 0.0)
    to_west = jnp.minimum(w, 0.0)
    to_north = jnp.maximum(n, 0.0)
    to_south = jnp.minimum(pltpu.roll(n, 1, 1), 0.0)
    centre = ((1.0 - to_east) + to_west) + (to_south - to_north)
    return centre, to_east, to_west, to_north, to_south


def advected(a, parts):
    centre, to_east, to_west, to_north, to_south = parts
    cols, rows = a.shape
    along = to_east * pltpu.roll(a, cols - 1, 0) - to_west * pltpu.roll(a, 1, 0)
    across = to_north * pltpu.roll(a, rows - 1, 1) - to_south * pltpu.roll(a, 1, 1)
    return centre * a + (along + across)


def chain_level(count, chain, i):
    up = where_am_i() == chain
    return jnp.where(up, i, 2 * count - 1 - i), jnp.where(up, i, count - 1 - i)


def coupling_level(count, chain, i):
    return jnp.where(where_am_i() == chain, i, 2 * count - 2 - i)


class Columns:
    def __init__(self, count, strengths, kinds, inverse, lower, ratio, middle, state):
        self.count, self.strengths, self.kinds = count, strengths, kinds
        self.inverse, self.lower, self.ratio = inverse, lower, ratio
        self.middle, self.state = middle, state
        self.zero = jnp.zeros(state.shape[3:], jnp.float32)

    def both(self, members):
        return [(chain, m) for chain in range(2) for m in range(members)]

    def factorise_and_sweep(self, coupling, source):
        def level(i, carry):
            out = []
            for chain in range(2):
                inward = coupling(chain, i)
                outward, pairs = carry[chain]
                now = []
                for m, amount in enumerate(source(chain, i)):
                    rest, before = pairs[m]
                    k_in = self.strengths[m] * inward[self.kinds[m]]
                    k_out = self.strengths[m] * outward[self.kinds[m]]
                    left = 1.0 + k_out * rest
                    inv = 1.0 / (left + k_in)
                    low = k_out * inv
                    swept = amount * inv + low * before
                    self.inverse[chain, m, i] = inv
                    self.lower[chain, m, i] = low
                    self.ratio[chain, m, i] = k_in * inv
                    self.state[chain, m, i] = swept
                    now.append((left * inv, swept))
                out.append((tuple(inward), tuple(now)))
            return tuple(out)

        zero = self.zero
        outward = tuple(zero for _ in range(max(self.kinds) + 1))
        start = (outward, tuple((zero, zero) for _ in self.strengths))
        ends = lax.fori_loop(0, self.count, level, (start, start), unroll=self.count)
        for m in range(len(self.strengths)):
            near, far = ends[0][1][m][0], ends[1][1][m][0]
            self.middle[m] = 1.0 / (near + self.ratio[0, m, self.count - 1] * far)

    def sweep(self, members):
        every = self.both(members)

        def level(i, carry):
            out = []
            for chain, m in every:
                before = self.lower[chain, m, i] * carry[len(out)]
                out.append(self.state[chain, m, i] * self.inverse[chain, m, i] + before)
                self.state[chain, m, i] = out[-1]
            return tuple(out)

        lax.fori_loop(0, self.count, level, tuple(self.zero for _ in every), unroll=self.count)

    def back(self, members):
        last = self.count - 1
        every = self.both(members)
        ends = []
        for chain, m in every:
            mine, others = self.state[chain, m, last], self.state[1 - chain, m, last]
            ends.append((mine + self.ratio[chain, m, last] * others) * self.middle[m])
        for end, (chain, m) in zip(ends, every):
            self.state[chain, m, last] = end

        def level(step, carry):
            i = last - 1 - step
            out = []
            for chain, m in every:
                after = self.ratio[chain, m, i] * carry[len(out)]
                out.append(self.state[chain, m, i] + after)
                self.state[chain, m, i] = out[-1]
            return tuple(out)

        lax.fori_loop(0, last, level, tuple(ends), unroll=last)


def boundary_kernel(
    factor,
    block_own,
    block_other,
    edge_own,
    edge_other,
    slots,
    forcing,
    outer,
    to_cross,
    to_same,
    total,
    diff,
    faces,
    inverse,
    lower,
    ratio,
    middle,
    state,
):
    count, cols, rows = block_own.shape[1:]
    tracers = block_own.shape[0] - 4
    band = where_am_i()
    place = sublane((cols, rows))
    at = lane((cols, rows))
    beyond = jnp.where(band == 0, cols - 1, 0)
    outside = place == beyond
    edge = cols - 1 - beyond
    first = ((place - edge + 1) & 7) < 4
    outside_far = ((place - beyond) & 7) == 4
    blocks = (block_own, block_other)
    edges = (edge_own, edge_other)

    def joined(x, y):
        return jnp.where(first, x, pltpu.roll(y, 4, 0))

    def assemble(i, carry):
        for chain in range(2):
            g, l = chain_level(count, chain, i)
            packed = edges[chain][l]
            t, d, e = [
                jnp.where(outside, turned(packed, -q), blocks[chain][q, l]) for q in range(3)
            ]
            total[g] = t
            diff[g] = d
            faces[count * chain + i] = e
        return carry

    lax.fori_loop(0, count, assemble, 0, unroll=count)

    add_soundings(slots, total, forcing)

    def coupling(chain, i):
        d = diff[coupling_level(count, chain, i)]
        return [joined(d, d)]

    def source(chain, i):
        g, l = chain_level(count, chain, i)
        packed = edges[chain][l]
        force = forcing[g]
        force = joined(force, force)
        amounts = []
        for tr in range(0, tracers, 2):
            near = jnp.where(outside, turned(packed, -3 - tr), blocks[chain][4 + tr, l])
            far = pltpu.roll(blocks[chain][5 + tr, l], 4, 0)
            far = jnp.where(outside_far, turned(packed, -tr), far)
            amounts.append(jnp.where(first, near, far) + force)
        return amounts

    pairs = tracers // 2
    strengths = [jnp.where(first, factor[2 * m], factor[2 * m + 1]) for m in range(pairs)]
    columns = Columns(count, strengths, [0] * pairs, inverse, lower, ratio, middle, state)

    def advect(i, carry):
        for chain in range(2):
            _, l = chain_level(count, chain, i)
            e = faces[count * chain + i]
            n = jnp.where(at == rows - 1, 0.0, blocks[chain][3, l])
            e, n = joined(e, e), joined(n, n)
            parts = face_parts(e, pltpu.roll(e, 1, 0), n)
            for m in range(pairs):
                state[chain, m, i] = advected(state[chain, m, i], parts)
        return carry

    columns.factorise_and_sweep(coupling, source)
    columns.back(pairs)
    lax.fori_loop(0, count, advect, 0, unroll=count)
    columns.sweep(pairs)
    columns.back(pairs)

    def hand_out(j, carry):
        for chain, out in ((1, to_cross), (0, to_same)):
            one = state[chain, 0, 2 * j]
            for q, (m, side) in enumerate(((0, 0), (0, 1), (1, 0), (1, 1))):
                if q:
                    row = pltpu.roll(state[chain, m, 2 * j + side], q, 0)
                    one = jnp.where(((place - edge) & 3) == q, row, one)
            out[j] = one
        return carry

    lax.fori_loop(0, count // 2, hand_out, 0, unroll=count // 2)

    slot = (place - beyond) & 7

    def hand_over(i, carry):
        for chain in range(2):
            g, l = chain_level(count, chain, i)
            force = forcing[g]
            row = jnp.where(band == 0, force[cols - 1 : cols], force[0:1])
            tile = turned(edges[chain][l], -3)
            tile = jnp.where(slot < tracers, tile + row, tile)
            tile = jnp.where(slot == 4, turned(diff[coupling_level(count, chain, i)], 4), tile)
            near = jnp.where(band == 0, turned(force, 4), turned(force, 6))
            outer[count * chain + i] = jnp.where(slot == 5, near, tile)
        return carry

    lax.fori_loop(0, count, hand_over, 0, unroll=count)


def column_kernel(
    factor,
    block_own,
    block_other,
    forcing,
    outer,
    outer_other,
    inner,
    sides,
    inverse,
    lower,
    ratio,
    middle,
    state,
):
    tracers, count, cols, rows = inner.shape
    band = where_am_i()
    place = sublane((cols, rows))
    at = lane((cols, rows))
    beyond = jnp.where(band == 0, cols - 1, 0)
    slot = (place - beyond) & 7
    mine = slot < 4
    blocks = (block_own, block_other)

    def outers(chain, i):
        return outer[count * chain + i], outer_other[count * (1 - chain) + i]

    def coupling(chain, i):
        up = band == chain
        here = blocks[chain][1, jnp.where(up, i, jnp.maximum(count - 2 - i, 0))]
        across = jnp.logical_and(jnp.logical_not(up), i == count - 1)
        d = jnp.where(across, blocks[1 - chain][1, count - 1], here)
        own, got = outers(chain, i)
        d_own = jnp.where(band == 0, own[3:4], own[4:5])
        d_got = jnp.where(band == 0, got[4:5], got[3:4])
        return [d, jnp.where(mine, d_own, d_got)]

    def source(chain, i):
        g, l = chain_level(count, chain, i)
        own, got = outers(chain, i)
        force = jnp.where(
            place == beyond, jnp.where(band == 0, turned(got, 2), turned(got, 4)), forcing[g]
        )
        moved = jnp.where(band == 0, turned(got, 3), turned(got, 5))
        return [blocks[chain][4 + tr, l] + force for tr in range(tracers)] + [
            jnp.where(mine, own, moved)
        ]

    by_row = factor[0]
    for tr in range(1, tracers):
        by_row = jnp.where((slot & 3) == tr, factor[tr], by_row)
    strengths = [factor[tr] for tr in range(tracers)] + [by_row]
    kinds = [0] * tracers + [1]
    columns = Columns(count, strengths, kinds, inverse, lower, ratio, middle, state)

    def parts_of(chain, i):
        _, l = chain_level(count, chain, i)
        own, got = outers(chain, i)
        e = blocks[chain][2, l]
        n = jnp.where(at == rows - 1, 0.0, blocks[chain][3, l])
        before = turned(jnp.where(band == 0, own, got), 2)
        return face_parts(e, jnp.where(place == 0, before, pltpu.roll(e, 1, 0)), n)

    def advect(i, carry):
        for chain in range(2):
            centre, to_east, to_west, to_north, to_south = parts_of(chain, i)
            around = state[chain, tracers, i]
            west = jnp.where(band == 0, around, turned(around, 3))
            east = jnp.where(band == 0, turned(around, 5), around)
            for tr in range(tracers):
                a = state[chain, tr, i]
                a_east = jnp.where(
                    place == cols - 1, turned(east, -1 - tr), pltpu.roll(a, cols - 1, 0)
                )
                a_west = jnp.where(place == 0, turned(west, 1 - tr), pltpu.roll(a, 1, 0))
                along = to_east * a_east - to_west * a_west
                across = to_north * pltpu.roll(a, rows - 1, 1) - to_south * pltpu.roll(a, 1, 1)
                state[chain, tr, i] = centre * a + (along + across)
        return carry

    columns.factorise_and_sweep(coupling, source)
    columns.back(tracers + 1)
    lax.fori_loop(0, count, advect, 0, unroll=count)
    columns.sweep(tracers)
    columns.back(tracers)

    def last(i, carry):
        _, l = chain_level(count, 0, i)
        centre, to_east, to_west, to_north, to_south = parts_of(0, i)
        sides[i] = jnp.where(
            place == cols - 1, to_east, jnp.where(place == 0, -to_west, 0.0)
        )
        to_east = jnp.where(place == cols - 1, 0.0, to_east)
        to_west = jnp.where(place == 0, 0.0, to_west)
        for tr in range(tracers):
            parts = (centre, to_east, to_west, to_north, to_south)
            inner[tr, l] = advected(state[0, tr, i], parts)
        return carry

    lax.fori_loop(0, count, last, 0, unroll=count)


def border_kernel(inner, sides, from_cross, from_same, out, ready, done):
    tracers, count, cols, rows = inner.shape
    band = where_am_i()
    place = sublane((cols, rows))
    copies = []
    for j in range(count // 2):
        cross, same = from_cross[j], from_same[j]
        westward = jnp.where(band == 0, cross, same)
        eastward = jnp.where(band == 0, same, cross)
        for side in range(2):
            i = 2 * j + side
            l = jnp.where(band == 0, i, count - 1 - i)
            for tr in range(tracers):
                q = 4 * (tr & 1) + 2 * (tr >> 1) + side
                beyond = jnp.where(place == 0, turned(westward, 1 - q), turned(eastward, -1 - q))
                ready[tr, l] = inner[tr, l] + sides[i] * beyond
        low = jnp.where(band == 0, 2 * j, count - 2 - 2 * j)
        part = (slice(None), pl.ds(low, 2))
        copies.append(pltpu.make_async_copy(ready.at[part], out.at[part], done.at[j]))
        copies[-1].start()
    for copy in copies:
        copy.wait()


def f32(*shape):
    return jax.ShapeDtypeStruct(shape, jnp.float32)


def call(kernel, outs, scratch, ops, limit, smem=0, moved=None, out_space=pltpu.VMEM):
    vmem = pl.BlockSpec(memory_space=pltpu.VMEM)
    scalars = pl.BlockSpec(memory_space=pltpu.SMEM)

    def run(*args):
        size = moved or sum(4 * a.size for a in args) + sum(4 * o.size for o in outs)
        return pl.pallas_call(
            kernel,
            out_shape=outs,
            in_specs=[scalars] * smem + [vmem] * (len(args) - smem),
            out_specs=[pl.BlockSpec(memory_space=out_space)] * len(outs),
            scratch_shapes=scratch,
            compiler_params=pltpu.CompilerParams(vmem_limit_bytes=limit * MIB),
            cost_estimate=pl.CostEstimate(flops=ops, bytes_accessed=size, transcendentals=0),
        )(*args)

    return run


def per_device(
    tiles,
    concentration,
    adjoint_later,
    courant_east,
    courant_north,
    diffusivity,
    tracer_factor,
    sounding_cell,
    sounding_value,
    sounding_precision,
    sounding_weight,
):
    tracers, band_levels, cols, rows = concentration.shape
    levels = 2 * band_levels
    blocks = sounding_cell.shape[0] // LANES
    field = f32(band_levels, cols, rows)
    deep = f32(levels, cols, rows)

    first = call(first_kernel, [f32(8, LANES)], [], 10**9, 8)()[0]
    block, edge_same, edge_cross, message = call(
        pack_kernel,
        [f32(4 + tracers, band_levels, cols, rows), field, field, f32(tiles, 8, LANES)],
        [pltpu.VMEM((4, blocks, 8, LANES), jnp.float32)],
        10**6,
        16,
    )(
        first,
        concentration,
        adjoint_later,
        courant_east,
        courant_north,
        diffusivity,
        sounding_cell.reshape(blocks, LANES),
        sounding_value.reshape(blocks, LANES),
        sounding_precision.reshape(blocks, LANES),
        sounding_weight.T,
    )

    both = ("tile", "band")
    same = [(2 * t, 2 * ((t + 1) % tiles)) for t in range(tiles)]
    same += [(2 * t + 1, 2 * ((t - 1) % tiles) + 1) for t in range(tiles)]
    cross = [(2 * t + 1, 2 * ((t + 1) % tiles)) for t in range(tiles)]
    cross += [(2 * t, 2 * ((t - 1) % tiles) + 1) for t in range(tiles)]
    along = [(2 * t + 1, 2 * ((t + 1) % tiles) + 1) for t in range(tiles)]
    along += [(2 * t, 2 * ((t - 1) % tiles)) for t in range(tiles)]
    swap = [(0, 1), (1, 0)]

    edge_own = lax.ppermute(edge_same, both, same)
    edge_other = lax.ppermute(edge_cross, both, cross)
    block_other = lax.ppermute(block, "band", swap)
    slots = lax.all_to_all(
        message.reshape(2 * tiles, 4, LANES), both, split_axis=0, concat_axis=0, tiled=True
    ).reshape(tiles, 8, LANES)

    part = f32(band_levels // 2, cols, rows)
    whole = f32(tracers, band_levels, cols, rows)

    def room(members):
        chains = pltpu.VMEM((2, members, band_levels, cols, rows), jnp.float32)
        return [chains] * 3 + [pltpu.VMEM((members, cols, rows), jnp.float32), chains]

    forcing, outer, to_cross, to_same = call(
        boundary_kernel,
        [deep, deep, part, part],
        [pltpu.VMEM((levels, cols, rows), jnp.float32)] * 3 + room(tracers // 2),
        10**8,
        24,
        smem=1,
    )(tracer_factor, block, block_other, edge_own, edge_other, slots)
    from_cross = lax.ppermute(to_cross, both, cross)
    from_same = lax.ppermute(to_same, both, along)
    outer_other = lax.ppermute(outer, "band", swap)
    inner, sides = call(
        column_kernel, [whole, field], room(tracers + 1), 10**9, 24, smem=1
    )(tracer_factor, block, block_other, forcing, outer, outer_other)
    ready = pltpu.VMEM((tracers, band_levels, cols, rows), jnp.float32)
    done = pltpu.SemaphoreType.DMA((band_levels // 2,))
    return call(border_kernel, [whole], [ready, done], 10**6, 16, out_space=pl.ANY)(
        inner, sides, from_cross, from_same
    )[0]


def solution(mesh):
    return jax.shard_map(
        functools.partial(per_device, mesh.shape["tile"]),
        mesh=mesh,
        in_specs=(
            P(None, "band", "tile", None),
            P(None, "band", "tile", None),
            P("band", "tile", None),
            P("band", "tile", None),
            P("band", "tile", None),
            P(),
            P("tile"),
            P("tile"),
            P("tile"),
            P("tile", "band"),
        ),
        out_specs=P(None, "band", "tile", None),
        check_vma=False,
    )
```
